128 devices in a mesh: section: 8 (over x, core), tensor: 16 (over y, z).
Axes of the slice: x: 4, y: 4, z: 4, core: 2. Of those that a mesh axis runs over, the one named last changes fastest.
Arguments:
- hidden: bfloat16 [512, 4608], P(('section', 'tensor')), may hold values from -0.59765625 to 0.59765625
- norm_gain: float32 [4608], replicated, may hold values from 0.5 to 1.5
- head_weight: bfloat16 [128000, 4608], P(('section', 'tensor')), as said below
- targets: int32 [512], replicated, may hold values from 0 to 127999
Outputs:
- token_loss: float32 [512], P(('section', 'tensor'))
- grad_gain: float32 [4608], replicated
- grad_hidden: float32 [512, 4608], P(('section', 'tensor'))
- grad_head: bfloat16 [128000, 4608], P(('section', 'tensor'))
The draws below stay inside these ranges and needn't reach their ends.
Inputs may be any that keep to these rules, and one draw needn't show every extreme that they name: head_weight entries are finite and at most 19.5 times 4608^-0.5 in magnitude.
All inputs are finite; a program needn't handle non-finite values.
Results may differ from the reference program's by a relative error of at most 0.0054.
Values may be sent and summed in bfloat16 or wider, within the bound.
No kernel may reach another device: no remote copies, remote signals or barrier semaphores. Data moves between devices by JAX's collectives and lax.ppermute only.
A program may use at most 128 MiB of HBM per device.

```python
import jax
import jax.numpy as jnp
from jax import lax

D = 4608
VOCAB = 128000
TOKENS = 512


def draw_head_weight(key, part):
    key = jax.random.fold_in(key, 11)
    first_key = jax.random.fold_in(key, 0)
    position = jnp.arange(VOCAB, dtype=jnp.float32)
    row_scale = 3.0 / jnp.sqrt(jnp.float32(D)) * (0.8 + 0.4 * position / VOCAB)
    values = jnp.clip(jax.random.normal(first_key, (VOCAB, D), jnp.float32), -5.4, 5.4) * row_scale[:, None]
    return values.astype(jnp.bfloat16)


def place_ends(array, own_key, smallest, largest):
    dims = array.shape
    index_at = [jax.random.randint(jax.random.fold_in(own_key, axis), (), 0, dims[axis]) for axis in range(len(dims))]
    array = array.at[tuple(index_at)].set(smallest)
    longest = dims.index(max(dims))
    index_at[longest] = (index_at[longest] + 1) % dims[longest]
    return array.at[tuple(index_at)].set(largest)


def level_of(own_key, dims, shards, low, top_value):
    gain = 1.0
    for dim, parts in shards:
        heights = jax.random.uniform(jax.random.fold_in(jax.random.fold_in(own_key, 6), dim), (parts,), jnp.float32, low / len(shards), top_value / len(shards))
        gain = gain * jnp.repeat(jnp.exp(heights), dims[dim] // parts).reshape((-1,) + (1,) * (len(dims) - 1 - dim))
    return gain


def centred(stream_key, shape, scale, most, shards=(), kind=jnp.bfloat16):
    entries = scale * jax.random.normal(stream_key, shape, jnp.float32)
    if shards:
        entries = entries * level_of(stream_key, shape, shards, -0.22, 0.18)
    return jnp.clip(entries, -most, most).astype(kind)


def setup_inputs(seed: int = 0) -> dict:
    keys = jax.random.split(jax.random.key(seed), 5)
    return {
        "hidden": centred(keys[0], (TOKENS, D), 0.1, 0.59765625, ((0, 128),)),
        "norm_gain": jnp.clip(1.0 + 0.1 * jax.random.normal(keys[1], (D,), jnp.float32), 0.5, 1.5),
        "head_weight": draw_head_weight(jax.random.fold_in(keys[4], 71), 0),
        "targets": place_ends(jax.random.randint(keys[3], (TOKENS,), 0, VOCAB), jax.random.fold_in(keys[3], 1), 0, VOCAB - 1).astype(jnp.int32),
    }


soft_cap = 30.0
norm_eps = 1e-06

def reference(hidden, norm_gain, head_weight, targets):
    values = hidden.astype(jnp.float32)
    root_mean = jnp.sqrt(lax.optimization_barrier(jnp.mean(values * values, axis=1, keepdims=True)) + norm_eps)
    unit_rows = values / root_mean
    normed = (unit_rows * norm_gain[None, :]).astype(jnp.bfloat16)
    raw_logits = lax.dot_general(normed, head_weight, (((1,), (1,)), ((), ())), preferred_element_type=jnp.float32)
    capped = soft_cap * jnp.tanh(raw_logits / soft_cap)
    scaled_exp = jnp.exp(capped)
    exp_total = lax.optimization_barrier(jnp.sum(scaled_exp, axis=1))
    columns = jnp.arange(VOCAB, dtype=jnp.int32)
    onehot = columns[None, :] == targets[:, None]
    picked = lax.optimization_barrier(jnp.sum(jnp.where(onehot, capped, jnp.zeros_like(capped)), axis=1))
    token_loss = jnp.log(exp_total) - picked
    cap_slope = 1.0 - (capped / soft_cap) ** 2
    dlogit = ((scaled_exp / exp_total[:, None] - onehot.astype(jnp.float32)) * cap_slope).astype(jnp.bfloat16)
    grad_head = lax.dot_general(dlogit, normed, (((0,), (0,)), ((), ())), preferred_element_type=jnp.float32).astype(jnp.bfloat16)
    grad_normed = jnp.dot(dlogit, head_weight, preferred_element_type=jnp.float32)
    grad_gain = lax.optimization_barrier(jnp.sum(grad_normed * unit_rows, axis=0))
    grad_unit = grad_normed * norm_gain[None, :]
    inner_mean = lax.optimization_barrier(jnp.mean(grad_unit * unit_rows, axis=1, keepdims=True))
    grad_hidden = (grad_unit - unit_rows * inner_mean) / root_mean
    return (token_loss, grad_gain, grad_hidden, grad_head)
```

```python
import functools

import jax
import jax.numpy as jnp
from jax import lax
from jax.experimental import pallas as pl
from jax.experimental.pallas import tpu as pltpu
from jax.sharding import Mesh
from jax.sharding import PartitionSpec as P

soft_cap = 30.0
norm_eps = 1e-06
f32 = jnp.float32
bf16 = jnp.bfloat16
every = ("x", "c", "y", "z")
chips = ("x", "y", "z")
n_chips = 64
tokens = 512
width = 4608
half = width // 2
tile = 768
tiles = half // tile
wide = tile + 128
vocab_tile = 256

swap_cores = [
    (((x * 2 + c) * 4 + y) * 4 + z, ((x * 2 + 1 - c) * 4 + y) * 4 + z)
    for x in range(4)
    for c in range(2)
    for y in range(4)
    for z in range(4)
]


def other_core(array):
    return lax.ppermute(array, every, swap_cores)


def params(flops=0, bytes_accessed=0, transcendentals=0):
    return dict(
        compiler_params=pltpu.CompilerParams(vmem_limit_bytes=48 << 20),
        cost_estimate=pl.CostEstimate(
            flops=flops, bytes_accessed=bytes_accessed, transcendentals=transcendentals
        ),
    )


def norm_kernel(core, mine, theirs, gain, spread, unit_out, root_out):
    first = core[0] == 0
    own = mine[...].astype(f32)
    far = theirs[...].astype(f32)
    rows = jnp.concatenate([jnp.where(first, own, far), jnp.where(first, far, own)], axis=0)
    root = jnp.sqrt(jnp.mean(rows * rows, axis=1, keepdims=True) + norm_eps)
    unit = rows / root
    normed = unit * gain[...]
    part = jnp.where(first, normed[:, :half], normed[:, half:]).astype(bf16)
    spread[...] = jnp.broadcast_to(part[None], spread.shape)
    unit_out[...] = jnp.where(first, unit[:4], unit[4:])
    root_out[...] = jnp.broadcast_to(jnp.where(first, root[:4], root[4:]), root_out.shape)


def logits_first_kernel(core, own, weight, out):
    out[...] = lax.dot_general(
        weight[...], own[...], (((1,), (1,)), ((), ())), preferred_element_type=f32
    )


def logits_kernel(vocab, core, other, weight, part, picks, capped_out, stats):
    step = pl.program_id(0)
    raw = part[...] + lax.dot_general(
        weight[...], other[...], (((1,), (1,)), ((), ())), preferred_element_type=f32
    )
    capped = soft_cap * jnp.tanh(raw / soft_cap)
    capped_out[...] = capped
    row = lax.broadcasted_iota(jnp.int32, capped.shape, 0) + step * vocab_tile
    total = jnp.sum(jnp.where(row < vocab, jnp.exp(capped), 0.0), axis=0, keepdims=True)
    hit = (row == picks[...]) & (row < vocab)
    picked = jnp.sum(jnp.where(hit, capped, 0.0), axis=0, keepdims=True)

    @pl.when(step == 0)
    def _():
        stats[...] = jnp.zeros_like(stats)

    for j in range(4):
        lanes = slice(128 * j, 128 * (j + 1))
        stats[j : j + 1, :] += total[:, lanes]
        stats[4 + j : 5 + j, :] += picked[:, lanes]


def far_grad_kernel(core, capped, total, picks, weight, normed, gain, grad_out, dlogit_out, gain_out):
    @pl.when(pl.program_id(0) == 0)
    def _():
        value = capped[...]
        row = lax.broadcasted_iota(jnp.int32, value.shape, 0)
        onehot = (row == picks[...]).astype(f32)
        slope = 1.0 - (value / soft_cap) ** 2
        dlogit_out[...] = ((jnp.exp(value) / total[...] - onehot) * slope).astype(bf16)

    grad = lax.dot_general(
        dlogit_out[...], weight[...], (((0,), (0,)), ((), ())), preferred_element_type=f32
    )
    grad_out[...] = grad.astype(bf16)
    gain_out[...] = jnp.sum(grad * normed[...].astype(f32), axis=0, keepdims=True) / gain[...]


def head_kernel(core, dlogit, own, other, out):
    near = pl.program_id(0) // tiles == core[0]

    @pl.when(near)
    def _():
        out[...] = jnp.dot(dlogit[...], own[...], preferred_element_type=f32).astype(bf16)

    @pl.when(jnp.logical_not(near))
    def _():
        out[...] = jnp.dot(dlogit[...], other[...], preferred_element_type=f32).astype(bf16)


def near_grad_kernel(core, dlogit, weight, normed, gain, received, received_gain, out):
    grad = lax.dot_general(
        dlogit[...], weight[...], (((0,), (0,)), ((), ())), preferred_element_type=f32
    )
    out[:, :tile] = (grad + received[...].astype(f32)).astype(bf16)
    part = jnp.sum(grad * normed[...].astype(f32), axis=0, keepdims=True) / gain[...]
    part = part + received_gain[...]
    rows = [part[:, 128 * j : 128 * (j + 1)] for j in range(tile // 128)]
    rows = jnp.concatenate(rows + [jnp.zeros((8 - len(rows), 128), f32)], axis=0)
    rows = jnp.broadcast_to(rows[None], (n_chips, 8, 128)).reshape(n_chips * 8, 128)
    out[:, tile:] = rows.astype(bf16)


def sum_kernel(core, blocks, keep, send):
    total = jnp.sum(blocks[...].astype(f32), axis=0)
    first = core[0] == 0
    keep[...] = jnp.zeros_like(keep)
    send[...] = jnp.zeros_like(send)
    for j in range(tiles):
        lanes = slice(tile * j, tile * (j + 1))
        grad = total[:, wide * j : wide * j + tile]
        keep[0:4, lanes] = jnp.where(first, grad[:4], grad[4:])
        send[0:4, lanes] = jnp.where(first, grad[4:], grad[:4])
        for k in range(tile // 128):
            row = total[k : k + 1, wide * j + tile : wide * (j + 1)]
            lane = slice(tile * j + 128 * k, tile * j + 128 * (k + 1))
            keep[4:5, lane] = row
            send[4:5, lane] = row


def final_kernel(core, keep, received, unit, root, gain, grad_out, gain_out):
    first = core[0] == 0
    near, far = keep[...], received[...]
    both = jnp.concatenate([jnp.where(first, near, far), jnp.where(first, far, near)], axis=1)
    gain_out[...] = both[4:5]
    grad_unit = both[0:4] * gain[...]
    rows = unit[...]
    inner = jnp.mean(grad_unit * rows, axis=1, keepdims=True)
    grad_out[...] = (grad_unit - rows * inner) / root[:, 0:1]


def call(kernel, core, args, grid, in_specs, out_specs, out_shape, scratch=(), **cost):
    return pl.pallas_call(
        kernel,
        grid_spec=pltpu.PrefetchScalarGridSpec(
            num_scalar_prefetch=1,
            grid=grid,
            in_specs=in_specs,
            out_specs=out_specs,
            scratch_shapes=scratch,
        ),
        out_shape=out_shape,
        **params(**cost),
    )(core, *args)


def shape(dims, dtype):
    return jax.ShapeDtypeStruct(dims, dtype)


def whole(*dims):
    return pl.BlockSpec(dims, lambda *_: (0,) * len(dims))


def body(hidden, norm_gain, head_weight, targets):
    vocab = head_weight.shape[0]
    place = [lax.axis_index(name) for name in every]
    device = ((place[0] * 2 + place[1]) * 4 + place[2]) * 4 + place[3]
    core = place[1][None]
    gain = norm_gain[None, :]
    picks = targets.reshape(4, 2, 16, 4).transpose(0, 2, 1, 3).reshape(1, tokens) - device * vocab

    spread, unit, root = call(
        norm_kernel,
        core,
        (hidden, other_core(hidden), gain),
        (1,),
        [whole(4, width), whole(4, width), whole(1, width)],
        [whole(n_chips, 8, half), whole(4, width), whole(4, 128)],
        [shape((n_chips, 8, half), bf16), shape((4, width), f32), shape((4, 128), f32)],
    )
    own = lax.all_to_all(spread, chips, 0, 0, tiled=True).reshape(tokens, half)
    other = other_core(own)

    blocks = pl.cdiv(vocab, vocab_tile)
    logit_flops = 2 * tokens * vocab * half
    part = call(
        logits_first_kernel,
        core,
        (own, head_weight),
        (blocks,),
        [whole(tokens, half), pl.BlockSpec((vocab_tile, half), lambda i, c: (i, c[0]))],
        pl.BlockSpec((vocab_tile, tokens), lambda i, c: (i, 0)),
        shape((vocab, tokens), f32),
        flops=logit_flops,
        bytes_accessed=9 << 20,
    )
    capped, stats = call(
        functools.partial(logits_kernel, vocab),
        core,
        (other, head_weight, part, picks),
        (blocks,),
        [
            whole(tokens, half),
            pl.BlockSpec((vocab_tile, half), lambda i, c: (i, 1 - c[0])),
            pl.BlockSpec((vocab_tile, tokens), lambda i, c: (i, 0)),
            whole(1, tokens),
        ],
        [pl.BlockSpec((vocab_tile, tokens), lambda i, c: (i, 0)), whole(8, 128)],
        [shape((vocab, tokens), f32), shape((8, 128), f32)],
        flops=logit_flops,
        bytes_accessed=11 << 20,
    )
    stats = stats + other_core(stats)
    stats = jnp.broadcast_to(stats[None], (n_chips, 8, 128))
    stats = jnp.sum(lax.all_to_all(stats, chips, 0, 0, tiled=True), axis=0)
    total = stats[:4].reshape(1, tokens)
    loss = (jnp.log(stats[:4]) - stats[4:]).reshape(n_chips, 2, 4)
    chip = (place[0] * 4 + place[2]) * 4 + place[3]
    token_loss = lax.dynamic_slice(loss, (chip, place[1], 0), (1, 1, 4)).reshape(4)

    far_grad, dlogit, far_gain = call(
        far_grad_kernel,
        core,
        (capped, total, picks, head_weight, other, gain),
        (tiles,),
        [
            whole(vocab, tokens),
            whole(1, tokens),
            whole(1, tokens),
            pl.BlockSpec((vocab, tile), lambda j, c: (0, (1 - c[0]) * tiles + j)),
            pl.BlockSpec((tokens, tile), lambda j, c: (0, j)),
            pl.BlockSpec((1, tile), lambda j, c: (0, (1 - c[0]) * tiles + j)),
        ],
        [
            pl.BlockSpec((tokens, tile), lambda j, c: (0, j)),
            whole(vocab, tokens),
            pl.BlockSpec((1, tile), lambda j, c: (0, j)),
        ],
        [shape((tokens, half), bf16), shape((vocab, tokens), bf16), shape((1, half), f32)],
        flops=logit_flops,
        bytes_accessed=12 << 20,
    )
    received = other_core(far_grad)
    received_gain = other_core(far_gain)
    grad_head = call(
        head_kernel,
        core,
        (dlogit, own, other),
        (2 * tiles,),
        [
            whole(vocab, tokens),
            pl.BlockSpec((tokens, tile), lambda j, c: (0, jnp.clip(j - c[0] * tiles, 0, tiles - 1))),
            pl.BlockSpec(
                (tokens, tile), lambda j, c: (0, jnp.clip(j - (1 - c[0]) * tiles, 0, tiles - 1))
            ),
        ],
        pl.BlockSpec((vocab, tile), lambda j, c: (0, j)),
        shape((vocab, width), bf16),
        flops=2 * logit_flops,
        bytes_accessed=15 << 20,
    )
    packed = call(
        near_grad_kernel,
        core,
        (dlogit, head_weight, own, gain, received, received_gain),
        (tiles,),
        [
            whole(vocab, tokens),
            pl.BlockSpec((vocab, tile), lambda j, c: (0, c[0] * tiles + j)),
            pl.BlockSpec((tokens, tile), lambda j, c: (0, j)),
            pl.BlockSpec((1, tile), lambda j, c: (0, c[0] * tiles + j)),
            pl.BlockSpec((tokens, tile), lambda j, c: (0, j)),
            pl.BlockSpec((1, tile), lambda j, c: (0, j)),
        ],
        pl.BlockSpec((tokens, wide), lambda j, c: (0, j)),
        shape((tokens, tiles * wide), bf16),
        flops=logit_flops,
        bytes_accessed=13 << 20,
    )
    packed = packed.reshape(n_chips, 8, tiles * wide)
    packed = lax.all_to_all(packed, chips, 0, 0, tiled=True)
    keep, send = call(
        sum_kernel,
        core,
        (packed,),
        (1,),
        [whole(n_chips, 8, tiles * wide)],
        [whole(8, half), whole(8, half)],
        [shape((8, half), f32), shape((8, half), f32)],
    )
    grad_hidden, grad_gain = call(
        final_kernel,
        core,
        (keep, other_core(send), unit, root, gain),
        (1,),
        [whole(8, half), whole(8, half), whole(4, width), whole(4, 128), whole(1, width)],
        [whole(4, width), whole(1, width)],
        [shape((4, width), f32), shape((1, width), f32)],
    )
    return (token_loss, grad_gain.reshape(width), grad_hidden, grad_head)


def solution(mesh):
    fine = Mesh(mesh.devices.reshape(4, 2, 4, 4), every)
    rows = P(every, None)
    return jax.shard_map(
        body,
        mesh=fine,
        in_specs=(rows, P(), rows, P()),
        out_specs=(P(every), P(), rows, rows),
        check_vma=False,
    )
```

```python
import jax
import jax.numpy as jnp
from jax import lax
from jax.experimental import pallas as pl
from jax.experimental.pallas import tpu as pltpu
from jax.sharding import Mesh
from jax.sharding import PartitionSpec as P

soft_cap = 30.0
norm_eps = 1e-06
f32 = jnp.float32
bf16 = jnp.bfloat16
every = ("x", "c", "y", "z")
chips = ("x", "y", "z")
n_chips = 64
tokens = 512
width = 4608
half = width // 2
tile = 768
tiles = half // tile
wide = tile + 128

plane = 16
block = tokens // 4
chunk = 32
chunks = tokens // chunk
groups = ((0, 3), (1, 2))


def index(x, c, y, z):
    return ((x % 4 * 2 + c % 2) * 4 + y % 4) * 4 + z % 4


places = [(x, c, y, z) for x in range(4) for c in range(2) for y in range(4) for z in range(4)]
swap_cores = [(index(x, c, y, z), index(x, c + 1, y, z)) for x, c, y, z in places]
planes = [[index(x, 0, y, z) for y in range(4) for z in range(4)] for x in range(4)]
planes += [[index(x, 1, y, z) for x in range(4) for z in range(4)] for y in range(4)]


def other_core(array):
    return lax.ppermute(array, every, swap_cores)


def along_line(array, step):
    pairs = [
        (index(x, c, y, z), index(x + step * (1 - c), c, y + step * c, z)) for x, c, y, z in places
    ]
    return lax.ppermute(array, every, pairs)


def over_plane(array):
    return lax.all_to_all(array, every, 0, 0, axis_index_groups=planes, tiled=True)


def lane_rows(part):
    rows = [part[:, 128 * j : 128 * (j + 1)] for j in range(tile // 128)]
    return jnp.concatenate(rows + [jnp.zeros((8 - len(rows), 128), f32)], axis=0)


def assemble(table, blocks, out):
    for d in range(4):
        for k in range(4):
            row = pl.multiple_of(table(4 * d + k) * chunk, chunk)
            out[pl.ds(row, chunk), :] = blocks[d][chunk * k : chunk * (k + 1), :]


def params(room):
    return dict(
        compiler_params=pltpu.CompilerParams(vmem_limit_bytes=room << 20),
        cost_estimate=pl.CostEstimate(flops=1000, bytes_accessed=1000, transcendentals=0),
    )


def norm_kernel(core, mine, theirs, gain, spread, unit_out, root_out):
    first = core[0] == 0
    own = mine[...].astype(f32)
    far = theirs[...].astype(f32)
    rows = jnp.concatenate([jnp.where(first, own, far), jnp.where(first, far, own)], axis=0)
    root = jnp.sqrt(jnp.mean(rows * rows, axis=1, keepdims=True) + norm_eps)
    unit = rows / root
    normed = unit * gain[...]
    part = jnp.where(first, normed[:, :half], normed[:, half:]).astype(bf16)
    spread[...] = jnp.broadcast_to(part[None], spread.shape)
    unit_out[...] = jnp.where(first, unit[:4], unit[4:])
    root_out[...] = jnp.broadcast_to(jnp.where(first, root[:4], root[4:]), root_out.shape)


def half_of(weight, which):
    return weight[:, pl.ds(pl.multiple_of(which * half, half), half)]


def near_logits_kernel(core, b0, b1, weight, out, rows):
    rows[:block, :] = b0[...]
    rows[block:, :] = b1[...]
    out[...] = lax.dot_general(
        rows[...], half_of(weight, core[0]), (((1,), (1,)), ((), ())), preferred_element_type=f32
    )


def logits_kernel(core, b0, b1, b2, b3, weight, part0, part1, picks, out, stats, rows):
    assemble(lambda i: core[1 + chunks + i], (b0, b1, b2, b3), rows)
    out[...] = lax.dot_general(
        rows[...], half_of(weight, 1 - core[0]), (((1,), (1,)), ((), ())), preferred_element_type=f32
    )
    for g, part in enumerate((part0, part1)):
        for d in range(2):
            for k in range(4):
                row = pl.multiple_of(core[1 + 4 * groups[g][d] + k] * chunk, chunk)
                at = chunk * (4 * d + k)
                out[pl.ds(row, chunk), :] += part[at : at + chunk, :]
    for j in range(4):
        lines = slice(128 * j, 128 * (j + 1))
        capped = soft_cap * jnp.tanh(out[lines, :] / soft_cap)
        out[lines, :] = capped
        column = lax.broadcasted_iota(jnp.int32, capped.shape, 1)
        total = jnp.sum(jnp.exp(capped), axis=1, keepdims=True)
        picked = jnp.sum(jnp.where(column == picks[lines, :], capped, 0.0), axis=1, keepdims=True)
        stats[j : j + 1, :] = jnp.broadcast_to(total, (128, 128)).T[0:1, :]
        stats[4 + j : 5 + j, :] = jnp.broadcast_to(picked, (128, 128)).T[0:1, :]


def far_grad_kernel(core, capped, totals, picks, weight, out, dlogit):
    total = jnp.sum(totals[...], axis=0)
    for j in range(4):
        lines = slice(128 * j, 128 * (j + 1))
        column = jnp.broadcast_to(total[j : j + 1, :], (128, 128)).T[:, 0:1]
        value = capped[lines, :]
        onehot = (lax.broadcasted_iota(jnp.int32, value.shape, 1) == picks[lines, :]).astype(f32)
        slope = 1.0 - (value / soft_cap) ** 2
        dlogit[lines, :] = ((jnp.exp(value) / column - onehot) * slope).astype(bf16)
    out[...] = jnp.dot(
        dlogit[...], half_of(weight, 1 - core[0]), preferred_element_type=f32
    ).astype(bf16)


def near_grad_kernel(core, dlogit, weight, out):
    out[...] = jnp.dot(dlogit[...], half_of(weight, core[0]), preferred_element_type=f32)


def combine_kernel(core, grad, received, n0, n1, n2, n3, gain, o0, o1, o2, o3):
    for j in range(tiles):
        lanes = slice(tile * j, tile * (j + 1))
        part = jnp.zeros((8, tile), f32)
        for d, (out, normed) in enumerate(((o0, n0), (o1, n1), (o2, n2), (o3, n3))):
            for k in range(4):
                at = pl.ds(pl.multiple_of(core[1 + 4 * d + k] * chunk, chunk), chunk)
                rows = slice(chunk * k, chunk * (k + 1))
                value = grad[at, lanes] + received[at, lanes].astype(f32)
                out[rows, wide * j : wide * j + tile] = value.astype(bf16)
                value = value * normed[rows, lanes].astype(f32)
                part += jnp.sum(value.reshape(4, 8, tile), axis=0)
        spread = gain[:, pl.ds(pl.multiple_of(core[0] * half + tile * j, tile), tile)]
        sent = lane_rows(jnp.sum(part, axis=0, keepdims=True) / spread)
        sent = jnp.broadcast_to(sent[None], (plane, 8, 128)).reshape(block, 128).astype(bf16)
        for out in (o0, o1, o2, o3):
            out[:, wide * j + tile : wide * (j + 1)] = sent


def head_kernel(core, dlogit, n0, n1, n2, n3, m0, m1, m2, m3, out, turned, own, other):
    step = pl.program_id(0)

    @pl.when(step == 0)
    def _():
        turned[...] = dlogit[...].astype(f32).T.astype(bf16)
        for first, blocks, rows in ((1, (n0, n1, n2, n3), own), (1 + chunks, (m0, m1, m2, m3), other)):
            for d in range(4):
                for k in range(4):
                    row = pl.multiple_of(core[first + 4 * d + k] * chunk, chunk)
                    for j in range(tiles):
                        part = blocks[d][chunk * k : chunk * (k + 1), tile * j : tile * (j + 1)]
                        rows[j, pl.ds(row, chunk), :] = part

    near = step // tiles == core[0]

    @pl.when(near)
    def _():
        out[...] = jnp.dot(turned[...], own[step % tiles], preferred_element_type=f32).astype(bf16)

    @pl.when(jnp.logical_not(near))
    def _():
        out[...] = jnp.dot(turned[...], other[step % tiles], preferred_element_type=f32).astype(bf16)


def add_kernel(core, b0, b1, b2, b3, out):
    total = b0[...].astype(f32) + b1[...].astype(f32) + (b2[...].astype(f32) + b3[...].astype(f32))
    out[...] = total.astype(bf16)


def sum_kernel(core, blocks, keep, send):
    total = jnp.sum(blocks[...].astype(f32), axis=0)
    first = core[0] == 0
    keep[...] = jnp.zeros_like(keep)
    send[...] = jnp.zeros_like(send)
    for j in range(tiles):
        lanes = slice(tile * j, tile * (j + 1))
        grad = total[:, wide * j : wide * j + tile]
        keep[0:4, lanes] = jnp.where(first, grad[:4], grad[4:])
        send[0:4, lanes] = jnp.where(first, grad[4:], grad[:4])
        for k in range(tile // 128):
            row = total[k : k + 1, wide * j + tile : wide * (j + 1)]
            lane = slice(tile * j + 128 * k, tile * j + 128 * (k + 1))
            keep[4:5, lane] = row
            send[4:5, lane] = row


def final_kernel(core, keep, received, unit, root, gain, grad_out, gain_out):
    first = core[0] == 0
    near, far = keep[...], received[...]
    both = jnp.concatenate([jnp.where(first, near, far), jnp.where(first, far, near)], axis=1)
    gain_out[...] = both[4:5]
    grad_unit = both[0:4] * gain[...]
    rows = unit[...]
    inner = jnp.mean(grad_unit * rows, axis=1, keepdims=True)
    grad_out[...] = (grad_unit - rows * inner) / root[:, 0:1]


def call(kernel, core, args, out_shape, scratch=(), grid=(1,), out_specs=None, room=24):
    here = pl.BlockSpec(memory_space=pltpu.VMEM)
    return pl.pallas_call(
        kernel,
        grid_spec=pltpu.PrefetchScalarGridSpec(
            num_scalar_prefetch=1,
            grid=grid,
            in_specs=[here] * len(args),
            out_specs=out_specs or jax.tree.map(lambda _: here, out_shape),
            scratch_shapes=scratch,
        ),
        out_shape=out_shape,
        **params(room),
    )(core, *args)


def shape(dims, dtype):
    return jax.ShapeDtypeStruct(dims, dtype)


def body(hidden, norm_gain, head_weight, targets):
    vocab = head_weight.shape[0]
    place = [lax.axis_index(name) for name in every]
    device = ((place[0] * 2 + place[1]) * 4 + place[2]) * 4 + place[3]
    steps = jnp.arange(4, dtype=jnp.int32)
    by_x = ((place[0] + steps) % 4 * 4)[:, None] + steps[None, :]
    by_y = steps[None, :] * 4 + ((place[2] + steps) % 4)[:, None]
    first = place[1] == 0
    core = jnp.concatenate(
        [
            place[1][None],
            jnp.where(first, by_x, by_y).reshape(chunks),
            jnp.where(first, by_y, by_x).reshape(chunks),
        ]
    )
    gain = norm_gain[None, :]

    spread, unit, root = call(
        norm_kernel,
        core,
        (hidden, other_core(hidden), gain),
        [shape((plane, 8, half), bf16), shape((4, width), f32), shape((4, 128), f32)],
    )
    near = over_plane(spread).reshape(block, half)
    near = [near, *(along_line(near, -d) for d in (1, 2, 3))]
    local, late = lax.optimization_barrier((near[0], targets))
    picks = late.reshape(4, 2, 16, 4).transpose(0, 2, 1, 3).reshape(tokens, 1) - device * vocab
    local, picks = lax.optimization_barrier((local, picks))

    parts = []
    far = [None] * 4
    for group in groups:
        for d in group:
            far[d] = other_core(near[d])
        part = call(
            near_logits_kernel,
            core,
            (local if group[0] == 0 else near[group[0]], near[group[1]], head_weight),
            shape((2 * block, vocab), f32),
            [pltpu.VMEM((2 * block, half), bf16)],
        )
        parts.append(part)
        if group[0] == 0:
            parts[0], near[1], near[2] = lax.optimization_barrier((part, near[1], near[2]))
    capped, stats = call(
        logits_kernel,
        core,
        (*far, head_weight, *parts, picks),
        [shape((tokens, vocab), f32), shape((8, 128), f32)],
        [pltpu.VMEM((tokens, half), bf16)],
    )
    stats = stats + other_core(stats)
    stats = jnp.broadcast_to(stats[None], (n_chips, 8, 128))
    stats = lax.all_to_all(stats, chips, 0, 0, tiled=True)

    far_grad, dlogit = call(
        far_grad_kernel,
        core,
        (capped, stats, picks, head_weight),
        [shape((tokens, half), bf16), shape((tokens, vocab), bf16)],
    )
    received = other_core(far_grad)
    near_grad = call(near_grad_kernel, core, (dlogit, head_weight), shape((tokens, half), f32))
    sums = call(
        combine_kernel,
        core,
        (near_grad, received, *near, gain),
        [shape((block, tiles * wide), bf16)] * 4,
    )
    arrived = [along_line(sums[d], d) for d in (1, 2, 3)]
    dlogit, local = lax.optimization_barrier((dlogit, sums[0]))
    grad_head = call(
        head_kernel,
        core,
        (dlogit, *near, *far),
        shape((vocab, width), bf16),
        [
            pltpu.VMEM((vocab, tokens), bf16),
            pltpu.VMEM((tiles, tokens, tile), bf16),
            pltpu.VMEM((tiles, tokens, tile), bf16),
        ],
        grid=(2 * tiles,),
        out_specs=pl.BlockSpec((vocab, tile), lambda j, c: (0, j)),
    )
    grad_head, local = lax.optimization_barrier((grad_head, local))
    packed = call(add_kernel, core, (local, *arrived), shape((block, tiles * wide), bf16))
    packed = over_plane(packed.reshape(plane, 8, tiles * wide))

    stats = jnp.sum(stats, axis=0)
    loss = (jnp.log(stats[:4]) - stats[4:]).reshape(n_chips, 2, 4)
    chip = (place[0] * 4 + place[2]) * 4 + place[3]
    token_loss = lax.dynamic_slice(loss, (chip, place[1], 0), (1, 1, 4)).reshape(4)
    keep, send = call(sum_kernel, core, (packed,), [shape((8, half), f32)] * 2)
    grad_hidden, grad_gain = call(
        final_kernel,
        core,
        (keep, other_core(send), unit, root, gain),
        [shape((4, width), f32), shape((1, width), f32)],
    )
    return (token_loss, grad_gain.reshape(width), grad_hidden, grad_head)


def solution(mesh):
    fine = Mesh(mesh.devices.reshape(4, 2, 4, 4), every)
    rows = P(every, None)
    return jax.shard_map(
        body,
        mesh=fine,
        in_specs=(rows, P(), rows, P()),
        out_specs=(P(every), P(), rows, rows),
        check_vma=False,
    )
```

```python
import jax
import jax.numpy as jnp
from jax import lax
from jax.experimental import pallas as pl
from jax.experimental.pallas import tpu as pltpu
from jax.sharding import Mesh
from jax.sharding import PartitionSpec as P

soft_cap = 30.0
norm_eps = 1e-06
f32 = jnp.float32
bf16 = jnp.bfloat16
every = ("x", "c", "y", "z")
chips = ("x", "y", "z")
n_chips = 64
tokens = 512
width = 4608
half = width // 2
tile = 768
tiles = half // tile
wide = tile + 128

plane = 16
block = tokens // 4
chunk = 32
chunks = tokens // chunk


def index(x, c, y, z):
    return ((x % 4 * 2 + c % 2) * 4 + y % 4) * 4 + z % 4


places = [(x, c, y, z) for x in range(4) for c in range(2) for y in range(4) for z in range(4)]
swap_cores = [(index(x, c, y, z), index(x, c + 1, y, z)) for x, c, y, z in places]
planes = [[index(x, 0, y, z) for y in range(4) for z in range(4)] for x in range(4)]
planes += [[index(x, 1, y, z) for x in range(4) for z in range(4)] for y in range(4)]


def other_core(array):
    return lax.ppermute(array, every, swap_cores)


def along_line(array, step):
    pairs = [
        (index(x, c, y, z), index(x + step * (1 - c), c, y + step * c, z)) for x, c, y, z in places
    ]
    return lax.ppermute(array, every, pairs)


def over_plane(array):
    return lax.all_to_all(array, every, 0, 0, axis_index_groups=planes, tiled=True)


def lane_rows(part):
    rows = [part[:, 128 * j : 128 * (j + 1)] for j in range(tile // 128)]
    return jnp.concatenate(rows + [jnp.zeros((8 - len(rows), 128), f32)], axis=0)


def assemble(table, blocks, out):
    for d in range(4):
        for k in range(4):
            row = pl.multiple_of(table(4 * d + k) * chunk, chunk)
            out[pl.ds(row, chunk), :] = blocks[d][chunk * k : chunk * (k + 1), :]


def params(room):
    return dict(
        compiler_params=pltpu.CompilerParams(vmem_limit_bytes=room << 20),
        cost_estimate=pl.CostEstimate(flops=1000, bytes_accessed=1000, transcendentals=0),
    )


def norm_kernel(core, mine, theirs, gain, spread, unit_out, root_out, row):
    first = core[0] == 0
    own = mine[...].astype(f32)
    far = theirs[...].astype(f32)
    rows = jnp.concatenate([jnp.where(first, own, far), jnp.where(first, far, own)], axis=0)
    root = jnp.sqrt(jnp.mean(rows * rows, axis=1, keepdims=True) + norm_eps)
    unit = rows / root
    normed = unit * gain[...].reshape(1, width)
    part = jnp.where(first, normed[:, :half], normed[:, half:]).astype(bf16)
    row[...] = gain[...].reshape(1, width)
    spread[...] = jnp.broadcast_to(part[None], spread.shape)
    unit_out[...] = jnp.where(first, unit[:4], unit[4:])
    root_out[...] = jnp.broadcast_to(jnp.where(first, root[:4], root[4:]), root_out.shape)


def half_of(weight, which):
    return weight[:, pl.ds(pl.multiple_of(which * half, half), half)]


def turned_column(row):
    return jnp.broadcast_to(row, (128, 128)).T[:, 0:1]


def hits_of(labels, j, dims):
    label = turned_column(labels[j : j + 1, :].astype(f32)).astype(jnp.int32)
    return lax.broadcasted_iota(jnp.int32, dims, 1) == label


def onehot_rows(labels, vocab):
    rows = [hits_of(labels, j, (128, vocab)).astype(f32).astype(bf16) for j in range(4)]
    return jnp.concatenate(rows, axis=0)


def far_target_kernel(core, weight, labels, out):
    onehot = onehot_rows(labels, weight.shape[0])
    out[...] = jnp.dot(
        onehot, half_of(weight, 1 - core[0]), preferred_element_type=f32
    ).astype(bf16)


def near_logits_kernel(core, *refs):
    *blocks, weight, out, rows = refs
    for d, ref in enumerate(blocks):
        rows[block * d : block * (d + 1), :] = ref[...]
    out[...] = lax.dot_general(
        rows[...], half_of(weight, core[0]), (((1,), (1,)), ((), ())), preferred_element_type=f32
    )


def logits_kernel(core, b0, b1, b2, b3, weight, part0, part1, labels, out, stats, others, rows):
    assemble(lambda i: core[1 + chunks + i], (b0, b1, b2, b3), rows)
    out[...] = lax.dot_general(
        rows[...], half_of(weight, 1 - core[0]), (((1,), (1,)), ((), ())), preferred_element_type=f32
    )
    for i in range(chunks):
        row = pl.multiple_of(core[1 + i] * chunk, chunk)
        part = part0[chunk * i : chunk * (i + 1), :] if i < 4 else part1[chunk * (i - 4) : chunk * (i - 3), :]
        out[pl.ds(row, chunk), :] += part
    for j in range(4):
        lines = slice(128 * j, 128 * (j + 1))
        capped = soft_cap * jnp.tanh(out[lines, :] / soft_cap)
        out[lines, :] = capped
        hit = hits_of(labels, j, capped.shape)
        exps = jnp.exp(capped)
        slope = 1.0 - (capped / soft_cap) ** 2
        others[lines, :] = jnp.where(hit, 0.0, exps * slope).astype(bf16)
        total = jnp.sum(exps, axis=1, keepdims=True)
        picked = jnp.sum(jnp.where(hit, capped, 0.0), axis=1, keepdims=True)
        stats[j : j + 1, :] = jnp.broadcast_to(total, (128, 128)).T[0:1, :]
        stats[4 + j : 5 + j, :] = jnp.broadcast_to(picked, (128, 128)).T[0:1, :]


def far_grad_kernel(core, others, weight, out):
    grad = jnp.dot(others[...], half_of(weight, 1 - core[0]), preferred_element_type=f32)
    out[...] = grad.astype(bf16)


def combine_kernel(
    core, capped, stats, labels, weight, received, target, n0, n1, n2, n3, gain,
    o0, o1, o2, o3, loss, totals, dlogit, held, inverse, factor
):
    sums = jnp.sum(stats[...], axis=0)
    total, picked = sums[0:4, :], sums[4:8, :]
    totals[...] = total
    loss[...] = jnp.log(total) - picked
    slack = (jnp.exp(picked) / total - 1.0) * (1.0 - (picked / soft_cap) ** 2)
    scale = 1.0 / total
    for j in range(4):
        lines = slice(128 * j, 128 * (j + 1))
        inverse[lines, :] = turned_column(scale[j : j + 1, :])
        factor[lines, :] = turned_column(slack[j : j + 1, :])
        value = capped[lines, :]
        onehot = hits_of(labels, j, value.shape).astype(f32)
        slope = 1.0 - (value / soft_cap) ** 2
        share = jnp.exp(value) / turned_column(total[j : j + 1, :])
        dlogit[lines, :] = ((share - onehot) * slope).astype(bf16)
    for out in (o0, o1, o2, o3):
        out[:, half:] = jnp.zeros((block, 128), bf16)
    for j in range(tiles):
        lanes = slice(tile * j, tile * (j + 1))
        from_start = pl.ds(pl.multiple_of(core[0] * half + tile * j, tile), tile)
        held[...] = jnp.dot(dlogit[...], weight[:, from_start], preferred_element_type=f32)
        part = jnp.zeros((8, tile), f32)
        for d, (out, normed) in enumerate(((o0, n0), (o1, n1), (o2, n2), (o3, n3))):
            for k in range(4):
                at = pl.ds(pl.multiple_of(core[1 + 4 * d + k] * chunk, chunk), chunk)
                rows = slice(chunk * k, chunk * (k + 1))
                value = held[at, :] + received[at, lanes].astype(f32) * inverse[at, :]
                value += target[at, lanes].astype(f32) * factor[at, :]
                out[rows, lanes] = value.astype(bf16)
                value = value * normed[rows, lanes].astype(f32)
                part += jnp.sum(value.reshape(4, 8, tile), axis=0)
        sent = lane_rows(jnp.sum(part, axis=0, keepdims=True) / gain[:, from_start])
        high = sent.astype(bf16).astype(f32)
        sent = jnp.concatenate([high, sent - high], axis=0).astype(bf16)
        for out in (o0, o1, o2, o3):
            out[16 * j : 16 * (j + 1), half:] = sent


def head_kernel(core, capped, stats, labels, n0, n1, n2, n3, m0, m1, m2, m3, out, turned, own, other):
    step = pl.program_id(0)

    @pl.when(step == 0)
    def _():
        for j in range(4):
            lines = slice(128 * j, 128 * (j + 1))
            value = capped[lines, :].T
            row = lax.broadcasted_iota(jnp.int32, value.shape, 0)
            onehot = (row == labels[j : j + 1, :]).astype(f32)
            slope = 1.0 - (value / soft_cap) ** 2
            dlogit = (jnp.exp(value) / stats[j : j + 1, :] - onehot) * slope
            turned[:, lines] = dlogit.astype(bf16)
        for first, blocks, rows in ((1, (n0, n1, n2, n3), own), (1 + chunks, (m0, m1, m2, m3), other)):
            for d in range(4):
                for k in range(4):
                    row = pl.multiple_of(core[first + 4 * d + k] * chunk, chunk)
                    for j in range(tiles):
                        part = blocks[d][chunk * k : chunk * (k + 1), tile * j : tile * (j + 1)]
                        rows[j, pl.ds(row, chunk), :] = part

    near = step // tiles == core[0]

    @pl.when(near)
    def _():
        out[...] = jnp.dot(turned[...], own[step % tiles], preferred_element_type=f32).astype(bf16)

    @pl.when(jnp.logical_not(near))
    def _():
        out[...] = jnp.dot(turned[...], other[step % tiles], preferred_element_type=f32).astype(bf16)


def add_kernel(core, b0, b1, b2, b3, out):
    total = b0[...].astype(f32) + b1[...].astype(f32) + (b2[...].astype(f32) + b3[...].astype(f32))
    for j in range(tiles):
        out[:, wide * j : wide * j + tile] = total[:, tile * j : tile * (j + 1)].astype(bf16)
        rows = total[16 * j : 16 * j + 8, half:] + total[16 * j + 8 : 16 * j + 16, half:]
        rows = jnp.broadcast_to(rows[None], (plane, 8, 128)).reshape(block, 128)
        out[:, wide * j + tile : wide * (j + 1)] = rows.astype(bf16)


def sum_kernel(core, blocks, keep, send):
    total = jnp.sum(blocks[...].astype(f32), axis=0)
    first = core[0] == 0
    keep[...] = jnp.zeros_like(keep)
    send[...] = jnp.zeros_like(send)
    for j in range(tiles):
        lanes = slice(tile * j, tile * (j + 1))
        grad = total[:, wide * j : wide * j + tile]
        keep[0:4, lanes] = jnp.where(first, grad[:4], grad[4:])
        send[0:4, lanes] = jnp.where(first, grad[4:], grad[:4])
        for k in range(tile // 128):
            row = total[k : k + 1, wide * j + tile : wide * (j + 1)]
            lane = slice(tile * j + 128 * k, tile * j + 128 * (k + 1))
            keep[4:5, lane] = row
            send[4:5, lane] = row


def final_kernel(core, keep, received, unit, root, gain, loss, loss_out, grad_out, gain_out):
    line = loss[pl.ds(core[1 + 2 * chunks], 1), :]
    loss_out[...] = pltpu.roll(line, core[2 + 2 * chunks], 1)[0, :4]
    first = core[0] == 0
    near, far = keep[...], received[...]
    both = jnp.concatenate([jnp.where(first, near, far), jnp.where(first, far, near)], axis=1)
    gain_out[...] = both[4:5].reshape(width)
    grad_unit = both[0:4] * gain[...]
    rows = unit[...]
    inner = jnp.mean(grad_unit * rows, axis=1, keepdims=True)
    grad_out[...] = (grad_unit - rows * inner) / root[:, 0:1]


def call(kernel, core, args, out_shape, scratch=(), grid=(1,), out_specs=None, room=16):
    here = pl.BlockSpec(memory_space=pltpu.VMEM)
    return pl.pallas_call(
        kernel,
        grid_spec=pltpu.PrefetchScalarGridSpec(
            num_scalar_prefetch=1,
            grid=grid,
            in_specs=[here] * len(args),
            out_specs=out_specs or jax.tree.map(lambda _: here, out_shape),
            scratch_shapes=scratch,
        ),
        out_shape=out_shape,
        **params(room),
    )(core, *args)


def shape(dims, dtype):
    return jax.ShapeDtypeStruct(dims, dtype)


def body(hidden, norm_gain, weight, targets):
    vocab = weight.shape[0]
    place = [lax.axis_index(name) for name in every]
    device = ((place[0] * 2 + place[1]) * 4 + place[2]) * 4 + place[3]
    token = ((place[0] * 4 + place[2]) * 4 + place[3]) * 8 + place[1] * 4
    steps = jnp.arange(4, dtype=jnp.int32)
    by_x = ((place[0] + steps) % 4 * 4)[:, None] + steps[None, :]
    by_y = steps[None, :] * 4 + ((place[2] + steps) % 4)[:, None]
    first = place[1] == 0
    core = jnp.concatenate(
        [
            place[1][None],
            jnp.where(first, by_x, by_y).reshape(chunks),
            jnp.where(first, by_y, by_x).reshape(chunks),
            (token // 128)[None],
            ((128 - token % 128) % 128)[None],
        ]
    )
    gain = norm_gain

    labels = targets.reshape(4, 2, 16, 4).transpose(0, 2, 1, 3).reshape(4, 128) - device * vocab
    spread, unit, root, gain = call(
        norm_kernel,
        core,
        (hidden, other_core(hidden), gain),
        [
            shape((plane, 8, half), bf16),
            shape((4, width), f32),
            shape((4, 128), f32),
            shape((1, width), f32),
        ],
    )
    spread, labels = lax.optimization_barrier((spread, labels))
    near = over_plane(spread).reshape(block, half)
    near = [near, *(along_line(near, -d) for d in (1, 2, 3))]
    local, late = lax.optimization_barrier((near[0], labels))
    target = call(far_target_kernel, core, (weight, late), shape((tokens, half), bf16))
    local, target = lax.optimization_barrier((local, target))
    target = other_core(target)
    parts = []
    far = [None] * 4
    for group in ((0,), (1, 2, 3)):
        for d in group:
            far[d] = other_core(near[d])
        part = call(
            near_logits_kernel,
            core,
            (*(near[d] if d else local for d in group), weight),
            shape((len(group) * block, vocab), f32),
            [pltpu.VMEM((len(group) * block, half), bf16)],
        )
        if group[0] == 0:
            part, near[1], near[2], near[3] = lax.optimization_barrier((part, *near[1:]))
        parts.append(part)
    capped, stats, others = call(
        logits_kernel,
        core,
        (*far, weight, *parts, labels),
        [shape((tokens, vocab), f32), shape((8, 128), f32), shape((tokens, vocab), bf16)],
        [pltpu.VMEM((tokens, half), bf16)],
    )
    stats = stats + other_core(stats)
    far_grad = call(far_grad_kernel, core, (others, weight), shape((tokens, half), bf16))
    stats, far_grad = lax.optimization_barrier((stats, far_grad))
    received = other_core(far_grad)
    stats = jnp.broadcast_to(stats[None], (n_chips, 8, 128))
    stats = lax.all_to_all(stats, chips, 0, 0, tiled=True)
    *sums, loss, totals = call(
        combine_kernel,
        core,
        (capped, stats, labels, weight, received, target, *near, gain),
        [shape((block, half + 128), bf16)] * 4 + [shape((4, 128), f32)] * 2,
        [
            pltpu.VMEM((tokens, vocab), bf16),
            pltpu.VMEM((tokens, tile), f32),
            pltpu.VMEM((tokens, 1), f32),
            pltpu.VMEM((tokens, 1), f32),
        ],
    )
    arrived = [along_line(sums[d], d) for d in (1, 2, 3)]
    local = sums[0]
    grad_head = call(
        head_kernel,
        core,
        (capped, totals, labels, *near, *far),
        shape((vocab, width), bf16),
        [
            pltpu.VMEM((vocab, tokens), bf16),
            pltpu.VMEM((tiles, tokens, tile), bf16),
            pltpu.VMEM((tiles, tokens, tile), bf16),
        ],
        grid=(2 * tiles,),
        out_specs=pl.BlockSpec((vocab, tile), lambda j, c: (0, j)),
    )
    grad_head, local = lax.optimization_barrier((grad_head, local))
    packed = call(add_kernel, core, (local, *arrived), shape((block, tiles * wide), bf16))
    packed = over_plane(packed.reshape(plane, 8, tiles * wide))

    keep, send = call(sum_kernel, core, (packed,), [shape((8, half), f32)] * 2)
    token_loss, grad_hidden, grad_gain = call(
        final_kernel,
        core,
        (keep, other_core(send), unit, root, gain, loss),
        [shape((4,), f32), shape((4, width), f32), shape((width,), f32)],
    )
    return (token_loss, grad_gain, grad_hidden, grad_head)


def solution(mesh):
    fine = Mesh(mesh.devices.reshape(4, 2, 4, 4), every)
    rows = P(every, None)
    return jax.shard_map(
        body,
        mesh=fine,
        in_specs=(rows, P(), rows, P()),
        out_specs=(P(every), P(), rows, rows),
        check_vma=False,
    )
```

```python
import jax
import jax.numpy as jnp
from jax import lax
from jax.experimental import pallas as pl
from jax.experimental.pallas import tpu as pltpu
from jax.sharding import Mesh
from jax.sharding import PartitionSpec as P

soft_cap = 30.0
norm_eps = 1e-06
f32 = jnp.float32
bf16 = jnp.bfloat16
every = ("x", "c", "y", "z")
chips = ("x", "y", "z")
n_chips = 64
tokens = 512
width = 4608
half = width // 2
tile = 768
tiles = half // tile
wide = tile + 128

plane = 16
vocab_tile = 256
block = tokens // 4
chunk = 32
chunks = tokens // chunk


def index(x, c, y, z):
    return ((x % 4 * 2 + c % 2) * 4 + y % 4) * 4 + z % 4


places = [(x, c, y, z) for x in range(4) for c in range(2) for y in range(4) for z in range(4)]
swap_cores = [(index(x, c, y, z), index(x, c + 1, y, z)) for x, c, y, z in places]
planes = [[index(x, 0, y, z) for y in range(4) for z in range(4)] for x in range(4)]
planes += [[index(x, 1, y, z) for x in range(4) for z in range(4)] for y in range(4)]


def other_core(array):
    return lax.ppermute(array, every, swap_cores)


def along_line(array, step):
    pairs = [
        (index(x, c, y, z), index(x + step * (1 - c), c, y + step * c, z)) for x, c, y, z in places
    ]
    return lax.ppermute(array, every, pairs)


def over_plane(array):
    return lax.all_to_all(array, every, 0, 0, axis_index_groups=planes, tiled=True)


def lane_rows(part):
    rows = [part[:, 128 * j : 128 * (j + 1)] for j in range(tile // 128)]
    return jnp.concatenate(rows + [jnp.zeros((8 - len(rows), 128), f32)], axis=0)


def assemble(table, blocks, out):
    for d in range(4):
        for k in range(4):
            row = pl.multiple_of(table(4 * d + k) * chunk, chunk)
            out[pl.ds(row, chunk), :] = blocks[d][chunk * k : chunk * (k + 1), :]


def params(room):
    return dict(
        compiler_params=pltpu.CompilerParams(vmem_limit_bytes=room << 20),
        cost_estimate=pl.CostEstimate(flops=1000, bytes_accessed=1000, transcendentals=0),
    )


def norm_kernel(core, mine, theirs, gain, spread, unit_out, root_out, row):
    first = core[0] == 0
    own = mine[...].astype(f32)
    far = theirs[...].astype(f32)
    rows = jnp.concatenate([jnp.where(first, own, far), jnp.where(first, far, own)], axis=0)
    root = jnp.sqrt(jnp.mean(rows * rows, axis=1, keepdims=True) + norm_eps)
    unit = rows / root
    normed = unit * gain[...].reshape(1, width)
    part = jnp.where(first, normed[:, :half], normed[:, half:]).astype(bf16)
    row[...] = gain[...].reshape(1, width)
    spread[...] = jnp.broadcast_to(part[None], spread.shape)
    unit_out[...] = jnp.where(first, unit[:4], unit[4:])
    root_out[...] = jnp.broadcast_to(jnp.where(first, root[:4], root[4:]), root_out.shape)


def half_of(weight, which):
    return weight[:, pl.ds(pl.multiple_of(which * half, half), half)]


def turned_column(row):
    return jnp.broadcast_to(row, (128, 128)).T[:, 0:1]


def hits_of(labels, j, dims):
    label = turned_column(labels[j : j + 1, :].astype(f32)).astype(jnp.int32)
    return lax.broadcasted_iota(jnp.int32, dims, 1) == label


def onehot_rows(labels, vocab):
    rows = [hits_of(labels, j, (128, vocab)).astype(f32).astype(bf16) for j in range(4)]
    return jnp.concatenate(rows, axis=0)


def far_target_kernel(core, weight, labels, out):
    onehot = onehot_rows(labels, weight.shape[0])
    out[...] = jnp.dot(
        onehot, half_of(weight, 1 - core[0]), preferred_element_type=f32
    ).astype(bf16)


def near_logits_kernel(core, *refs):
    *blocks, weight, out, rows = refs
    for d, ref in enumerate(blocks):
        rows[block * d : block * (d + 1), :] = ref[...]
    out[...] = lax.dot_general(
        rows[...], half_of(weight, core[0]), (((1,), (1,)), ((), ())), preferred_element_type=f32
    )


def logits_kernel(
    core, b0, b1, b2, b3, weight, part0, part1, labels, out, stats, others, rows
):
    assemble(lambda i: core[1 + chunks + i], (b0, b1, b2, b3), rows)
    vocab = weight.shape[0]
    from_start = pl.ds(pl.multiple_of((1 - core[0]) * half, half), half)
    marks = [turned_column(labels[j : j + 1, :].astype(f32)).astype(jnp.int32) for j in range(4)]
    totals = [jnp.zeros((128, 1), f32)] * 4
    picks = [jnp.zeros((128, 1), f32)] * 4
    for start in range(0, vocab, vocab_tile):
        some = slice(start, min(start + vocab_tile, vocab))
        out[:, some] = lax.dot_general(
            rows[...], weight[some, from_start], (((1,), (1,)), ((), ())), preferred_element_type=f32
        )
        for i in range(chunks):
            row = pl.multiple_of(core[1 + i] * chunk, chunk)
            part, at = (part0, i) if i < 4 else (part1, i - 4)
            out[pl.ds(row, chunk), some] += part[chunk * at : chunk * (at + 1), some]
        for j in range(4):
            lines = slice(128 * j, 128 * (j + 1))
            capped = soft_cap * jnp.tanh(out[lines, some] / soft_cap)
            hit = lax.broadcasted_iota(jnp.int32, capped.shape, 1) + start == marks[j]
            exps = jnp.exp(capped)
            slope = 1.0 - (capped / soft_cap) ** 2
            rest = jnp.where(hit, 0.0, exps * slope)
            out[lines, some] = rest
            others[lines, some] = rest.astype(bf16)
            totals[j] = totals[j] + jnp.sum(exps, axis=1, keepdims=True)
            picked = jnp.where(hit, capped, 0.0)
            picks[j] = picks[j] + jnp.sum(picked, axis=1, keepdims=True)
    for j in range(4):
        stats[j : j + 1, :] = jnp.broadcast_to(totals[j], (128, 128)).T[0:1, :]
        stats[4 + j : 5 + j, :] = jnp.broadcast_to(picks[j], (128, 128)).T[0:1, :]


def far_grad_kernel(core, others, weight, out):
    grad = jnp.dot(others[...], half_of(weight, 1 - core[0]), preferred_element_type=f32)
    out[...] = grad.astype(bf16)


def combine_kernel(
    core, others, stats, labels, weight, received, target, n0, n1, n2, n3, gain,
    o0, o1, o2, o3, loss, marks, dlogit, held, inverse, factor
):
    sums = jnp.sum(stats[...], axis=0)
    total, picked = sums[0:4, :], sums[4:8, :]
    loss[...] = jnp.log(total) - picked
    slack = (jnp.exp(picked) / total - 1.0) * (1.0 - (picked / soft_cap) ** 2)
    scale = 1.0 / total
    marks[0:4, :] = scale
    marks[4:8, :] = slack
    for j in range(4):
        lines = slice(128 * j, 128 * (j + 1))
        inverse[lines, :] = turned_column(scale[j : j + 1, :])
        factor[lines, :] = turned_column(slack[j : j + 1, :])
        hit = hits_of(labels, j, (128, weight.shape[0]))
        rest = others[lines, :] * turned_column(scale[j : j + 1, :])
        dlogit[lines, :] = jnp.where(hit, turned_column(slack[j : j + 1, :]), rest).astype(bf16)
    for out in (o0, o1, o2, o3):
        out[:, half:] = jnp.zeros((block, 128), bf16)
    for j in range(tiles):
        lanes = slice(tile * j, tile * (j + 1))
        from_start = pl.ds(pl.multiple_of(core[0] * half + tile * j, tile), tile)
        held[j] = jnp.dot(dlogit[...], weight[:, from_start], preferred_element_type=f32)
        part = jnp.zeros((8, tile), f32)
        for d, (out, normed) in enumerate(((o0, n0), (o1, n1), (o2, n2), (o3, n3))):
            for k in range(4):
                at = pl.ds(pl.multiple_of(core[1 + 4 * d + k] * chunk, chunk), chunk)
                rows = slice(chunk * k, chunk * (k + 1))
                value = held[j, at, :] + received[at, lanes].astype(f32) * inverse[at, :]
                value += target[at, lanes].astype(f32) * factor[at, :]
                out[rows, lanes] = value.astype(bf16)
                value = value * normed[rows, lanes].astype(f32)
                part += jnp.sum(value.reshape(4, 8, tile), axis=0)
        sent = lane_rows(jnp.sum(part, axis=0, keepdims=True) / gain[:, from_start])
        high = sent.astype(bf16).astype(f32)
        sent = jnp.concatenate([high, sent - high], axis=0).astype(bf16)
        for out in (o0, o1, o2, o3):
            out[16 * j : 16 * (j + 1), half:] = sent


def head_kernel(core, others, marks, labels, n0, n1, n2, n3, m0, m1, m2, m3, out, turned, own, other):
    step = pl.program_id(0)

    @pl.when(step == 0)
    def _():
        for j in range(4):
            lines = slice(128 * j, 128 * (j + 1))
            rest = others[lines, :].T * marks[j : j + 1, :]
            hit = lax.broadcasted_iota(jnp.int32, rest.shape, 0) == labels[j : j + 1, :]
            turned[:, lines] = jnp.where(hit, marks[4 + j : 5 + j, :], rest).astype(bf16)
        for first, blocks, rows in ((1, (n0, n1, n2, n3), own), (1 + chunks, (m0, m1, m2, m3), other)):
            for d in range(4):
                for k in range(4):
                    row = pl.multiple_of(core[first + 4 * d + k] * chunk, chunk)
                    for j in range(tiles):
                        part = blocks[d][chunk * k : chunk * (k + 1), tile * j : tile * (j + 1)]
                        rows[j, pl.ds(row, chunk), :] = part

    near = step // tiles == core[0]

    @pl.when(near)
    def _():
        out[...] = jnp.dot(turned[...], own[step % tiles], preferred_element_type=f32).astype(bf16)

    @pl.when(jnp.logical_not(near))
    def _():
        out[...] = jnp.dot(turned[...], other[step % tiles], preferred_element_type=f32).astype(bf16)


def add_kernel(core, b0, b1, b2, b3, out):
    total = b0[...].astype(f32) + b1[...].astype(f32) + (b2[...].astype(f32) + b3[...].astype(f32))
    for j in range(tiles):
        out[:, wide * j : wide * j + tile] = total[:, tile * j : tile * (j + 1)].astype(bf16)
        rows = total[16 * j : 16 * j + 8, half:] + total[16 * j + 8 : 16 * j + 16, half:]
        rows = jnp.broadcast_to(rows[None], (plane, 8, 128)).reshape(block, 128)
        out[:, wide * j + tile : wide * (j + 1)] = rows.astype(bf16)


def sum_kernel(core, blocks, keep, send):
    total = jnp.sum(blocks[...].astype(f32), axis=0)
    first = core[0] == 0
    keep[...] = jnp.zeros_like(keep)
    send[...] = jnp.zeros_like(send)
    for j in range(tiles):
        lanes = slice(tile * j, tile * (j + 1))
        grad = total[:, wide * j : wide * j + tile]
        keep[0:4, lanes] = jnp.where(first, grad[:4], grad[4:])
        send[0:4, lanes] = jnp.where(first, grad[4:], grad[:4])
        for k in range(tile // 128):
            row = total[k : k + 1, wide * j + tile : wide * (j + 1)]
            lane = slice(tile * j + 128 * k, tile * j + 128 * (k + 1))
            keep[4:5, lane] = row
            send[4:5, lane] = row


def final_kernel(core, keep, received, unit, root, gain, loss, loss_out, grad_out, gain_out):
    line = loss[pl.ds(core[1 + 2 * chunks], 1), :]
    loss_out[...] = pltpu.roll(line, core[2 + 2 * chunks], 1)[0, :4]
    first = core[0] == 0
    near, far = keep[...], received[...]
    both = jnp.concatenate([jnp.where(first, near, far), jnp.where(first, far, near)], axis=1)
    gain_out[...] = both[4:5].reshape(width)
    grad_unit = both[0:4] * gain[...]
    rows = unit[...]
    inner = jnp.mean(grad_unit * rows, axis=1, keepdims=True)
    grad_out[...] = (grad_unit - rows * inner) / root[:, 0:1]


def call(kernel, core, args, out_shape, scratch=(), grid=(1,), out_specs=None, room=16):
    here = pl.BlockSpec(memory_space=pltpu.VMEM)
    return pl.pallas_call(
        kernel,
        grid_spec=pltpu.PrefetchScalarGridSpec(
            num_scalar_prefetch=1,
            grid=grid,
            in_specs=[here] * len(args),
            out_specs=out_specs or jax.tree.map(lambda _: here, out_shape),
            scratch_shapes=scratch,
        ),
        out_shape=out_shape,
        **params(room),
    )(core, *args)


def shape(dims, dtype):
    return jax.ShapeDtypeStruct(dims, dtype)


def body(hidden, norm_gain, weight, targets):
    vocab = weight.shape[0]
    place = [lax.axis_index(name) for name in every]
    device = ((place[0] * 2 + place[1]) * 4 + place[2]) * 4 + place[3]
    token = ((place[0] * 4 + place[2]) * 4 + place[3]) * 8 + place[1] * 4
    steps = jnp.arange(4, dtype=jnp.int32)
    by_x = ((place[0] + steps) % 4 * 4)[:, None] + steps[None, :]
    by_y = steps[None, :] * 4 + ((place[2] + steps) % 4)[:, None]
    first = place[1] == 0
    core = jnp.concatenate(
        [
            place[1][None],
            jnp.where(first, by_x, by_y).reshape(chunks),
            jnp.where(first, by_y, by_x).reshape(chunks),
            (token // 128)[None],
            ((128 - token % 128) % 128)[None],
        ]
    )
    gain = norm_gain

    labels = targets.reshape(4, 2, 16, 4).transpose(0, 2, 1, 3).reshape(4, 128) - device * vocab
    spread, unit, root, gain = call(
        norm_kernel,
        core,
        (hidden, other_core(hidden), gain),
        [
            shape((plane, 8, half), bf16),
            shape((4, width), f32),
            shape((4, 128), f32),
            shape((1, width), f32),
        ],
    )
    spread, labels = lax.optimization_barrier((spread, labels))
    near = over_plane(spread).reshape(block, half)
    sent = {d: along_line(near, -d) for d in (2, 1, 3)}
    near = [near, sent[1], sent[2], sent[3]]
    local, late = lax.optimization_barrier((near[0], labels))
    target = call(far_target_kernel, core, (weight, late), shape((tokens, half), bf16))
    local, target = lax.optimization_barrier((local, target))
    target = other_core(target)
    parts = []
    far = [None] * 4
    for group in ((0,), (1, 2, 3)):
        for d in (0,) if group == (0,) else (2, 1, 3):
            far[d] = other_core(near[d])
        part = call(
            near_logits_kernel,
            core,
            (*(near[d] if d else local for d in group), weight),
            shape((len(group) * block, vocab), f32),
            [pltpu.VMEM((len(group) * block, half), bf16)],
        )
        if group[0] == 0:
            part, near[2], near[1], near[3] = lax.optimization_barrier(
                (part, near[2], near[1], near[3])
            )
        parts.append(part)
    rest, stats, others = call(
        logits_kernel,
        core,
        (*far, weight, *parts, labels),
        [shape((tokens, vocab), f32), shape((8, 128), f32), shape((tokens, vocab), bf16)],
        [pltpu.VMEM((tokens, half), bf16)],
    )
    stats = stats + other_core(stats)
    far_grad = call(far_grad_kernel, core, (others, weight), shape((tokens, half), bf16))
    stats, far_grad = lax.optimization_barrier((stats, far_grad))
    received = other_core(far_grad)
    stats = jnp.broadcast_to(stats[None], (n_chips, 8, 128))
    stats = lax.all_to_all(stats, chips, 0, 0, tiled=True)
    *sums, loss, marks = call(
        combine_kernel,
        core,
        (rest, stats, labels, weight, received, target, *near, gain),
        [shape((block, half + 128), bf16)] * 4 + [shape((4, 128), f32), shape((8, 128), f32)],
        [
            pltpu.VMEM((tokens, vocab), bf16),
            pltpu.VMEM((tiles, tokens, tile), f32),
            pltpu.VMEM((tokens, 1), f32),
            pltpu.VMEM((tokens, 1), f32),
        ],
    )
    arrived = [along_line(sums[d], d) for d in (1, 3, 2)]
    local = sums[0]
    grad_head = call(
        head_kernel,
        core,
        (rest, marks, labels, *near, *far),
        shape((vocab, width), bf16),
        [
            pltpu.VMEM((vocab, tokens), bf16),
            pltpu.VMEM((tiles, tokens, tile), bf16),
            pltpu.VMEM((tiles, tokens, tile), bf16),
        ],
        grid=(2 * tiles,),
        out_specs=pl.BlockSpec((vocab, tile), lambda j, c: (0, j)),
    )
    grad_head, local = lax.optimization_barrier((grad_head, local))
    packed = call(add_kernel, core, (local, *arrived), shape((block, tiles * wide), bf16))
    packed = over_plane(packed.reshape(plane, 8, tiles * wide))

    keep, send = call(sum_kernel, core, (packed,), [shape((8, half), f32)] * 2)
    token_loss, grad_hidden, grad_gain = call(
        final_kernel,
        core,
        (keep, other_core(send), unit, root, gain, loss),
        [shape((4,), f32), shape((4, width), f32), shape((width,), f32)],
    )
    return (token_loss, grad_gain, grad_hidden, grad_head)


def solution(mesh):
    fine = Mesh(mesh.devices.reshape(4, 2, 4, 4), every)
    rows = P(every, None)
    return jax.shard_map(
        body,
        mesh=fine,
        in_specs=(rows, P(), rows, P()),
        out_specs=(P(every), P(), rows, rows),
        check_vma=False,
    )
```

```python
import jax
import jax.numpy as jnp
from jax import lax
from jax.experimental import pallas as pl
from jax.experimental.pallas import tpu as pltpu
from jax.sharding import Mesh
from jax.sharding import PartitionSpec as P

soft_cap = 30.0
norm_eps = 1e-06
f32 = jnp.float32
bf16 = jnp.bfloat16
every = ("x", "c", "y", "z")
chips = ("x", "y", "z")
n_chips = 64
tokens = 512
width = 4608
half = width // 2
tile = 768
tiles = half // tile
wide = tile + 128

plane = 16
vocab_tile = 256
block = tokens // 4
chunk = 32
chunks = tokens // chunk


def index(x, c, y, z):
    return ((x % 4 * 2 + c % 2) * 4 + y % 4) * 4 + z % 4


places = [(x, c, y, z) for x in range(4) for c in range(2) for y in range(4) for z in range(4)]
swap_cores = [(index(x, c, y, z), index(x, c + 1, y, z)) for x, c, y, z in places]
planes = [[index(x, 0, y, z) for y in range(4) for z in range(4)] for x in range(4)]
planes += [[index(x, 1, y, z) for x in range(4) for z in range(4)] for y in range(4)]


def other_core(array):
    return lax.ppermute(array, every, swap_cores)


def along_line(array, step):
    pairs = [
        (index(x, c, y, z), index(x + step * (1 - c), c, y + step * c, z)) for x, c, y, z in places
    ]
    return lax.ppermute(array, every, pairs)


def over_plane(array):
    return lax.all_to_all(array, every, 0, 0, axis_index_groups=planes, tiled=True)


def lane_rows(part):
    rows = [part[:, 128 * j : 128 * (j + 1)] for j in range(tile // 128)]
    return jnp.concatenate(rows + [jnp.zeros((8 - len(rows), 128), f32)], axis=0)


def assemble(table, blocks, out):
    for d in range(4):
        for k in range(4):
            row = pl.multiple_of(table(4 * d + k) * chunk, chunk)
            out[pl.ds(row, chunk), :] = blocks[d][chunk * k : chunk * (k + 1), :]


def params(room):
    return dict(
        compiler_params=pltpu.CompilerParams(vmem_limit_bytes=room << 20),
        cost_estimate=pl.CostEstimate(flops=1000, bytes_accessed=1000, transcendentals=0),
    )


def norm_kernel(core, mine, theirs, gain, spread, unit_out, root_out, row):
    first = core[0] == 0
    own = mine[...].astype(f32)
    far = theirs[...].astype(f32)
    rows = jnp.concatenate([jnp.where(first, own, far), jnp.where(first, far, own)], axis=0)
    root = jnp.sqrt(jnp.mean(rows * rows, axis=1, keepdims=True) + norm_eps)
    unit = rows / root
    normed = unit * gain[...].reshape(1, width)
    part = jnp.where(first, normed[:, :half], normed[:, half:]).astype(bf16)
    row[...] = gain[...].reshape(1, width)
    spread[...] = jnp.broadcast_to(part[None], spread.shape)
    unit_out[...] = jnp.where(first, unit[:4], unit[4:])
    root_out[...] = jnp.broadcast_to(jnp.where(first, root[:4], root[4:]), root_out.shape)


def half_of(weight, which):
    return weight[:, pl.ds(pl.multiple_of(which * half, half), half)]


def turned_column(row):
    return jnp.broadcast_to(row, (128, 128)).T[:, 0:1]


def hits_of(labels, j, dims):
    label = turned_column(labels[j : j + 1, :].astype(f32)).astype(jnp.int32)
    return lax.broadcasted_iota(jnp.int32, dims, 1) == label


def onehot_rows(labels, vocab):
    rows = [hits_of(labels, j, (128, vocab)).astype(f32).astype(bf16) for j in range(4)]
    return jnp.concatenate(rows, axis=0)


def first_logits_kernel(core, weight, targets, b0, out, labels, part):
    to = lax.broadcasted_iota(jnp.int32, (128, 128), 1)
    source = ((to >> 2) & 1) * 64 + (to >> 3) * 4 + (to & 3)
    order = (lax.broadcasted_iota(jnp.int32, (128, 128), 0) == source).astype(f32)
    ids = jnp.concatenate([targets[...].astype(f32), jnp.zeros((4, 128), f32)], axis=0)
    ids = jnp.dot(ids, order, precision=lax.Precision.HIGHEST, preferred_element_type=f32)
    labels[...] = ids[:4].astype(jnp.int32) - core[3 + 2 * chunks]
    onehot = onehot_rows(labels, weight.shape[0])
    out[...] = jnp.dot(
        onehot, half_of(weight, 1 - core[0]), preferred_element_type=f32
    ).astype(bf16)
    part[...] = lax.dot_general(
        b0[...], half_of(weight, core[0]), (((1,), (1,)), ((), ())), preferred_element_type=f32
    )


def near_logits_kernel(core, *refs):
    *blocks, weight, out, rows = refs
    for d, ref in enumerate(blocks):
        rows[block * d : block * (d + 1), :] = ref[...]
    out[...] = lax.dot_general(
        rows[...], half_of(weight, core[0]), (((1,), (1,)), ((), ())), preferred_element_type=f32
    )


def logits_kernel(
    core, b0, b1, b2, b3, weight, part0, part1, labels, out, stats, others, rows
):
    assemble(lambda i: core[1 + chunks + i], (b0, b1, b2, b3), rows)
    vocab = weight.shape[0]
    from_start = pl.ds(pl.multiple_of((1 - core[0]) * half, half), half)
    marks = [turned_column(labels[j : j + 1, :].astype(f32)).astype(jnp.int32) for j in range(4)]
    totals = [jnp.zeros((128, 1), f32)] * 4
    picks = [jnp.zeros((128, 1), f32)] * 4
    for start in range(0, vocab, vocab_tile):
        some = slice(start, min(start + vocab_tile, vocab))
        out[:, some] = lax.dot_general(
            rows[...], weight[some, from_start], (((1,), (1,)), ((), ())), preferred_element_type=f32
        )
        for i in range(chunks):
            row = pl.multiple_of(core[1 + i] * chunk, chunk)
            part, at = (part0, i) if i < 4 else (part1, i - 4)
            out[pl.ds(row, chunk), some] += part[chunk * at : chunk * (at + 1), some]
        for j in range(4):
            lines = slice(128 * j, 128 * (j + 1))
            capped = soft_cap * jnp.tanh(out[lines, some] / soft_cap)
            hit = lax.broadcasted_iota(jnp.int32, capped.shape, 1) + start == marks[j]
            exps = jnp.exp(capped)
            slope = 1.0 - (capped / soft_cap) ** 2
            rest = jnp.where(hit, 0.0, exps * slope)
            out[lines, some] = rest
            others[lines, some] = rest.astype(bf16)
            totals[j] = totals[j] + jnp.sum(exps, axis=1, keepdims=True)
            picked = jnp.where(hit, capped, 0.0)
            picks[j] = picks[j] + jnp.sum(picked, axis=1, keepdims=True)
    for j in range(4):
        stats[j : j + 1, :] = jnp.broadcast_to(totals[j], (128, 128)).T[0:1, :]
        stats[4 + j : 5 + j, :] = jnp.broadcast_to(picks[j], (128, 128)).T[0:1, :]


def far_grad_kernel(core, others, weight, out):
    out[...] = jnp.dot(others[...], half_of(weight, 1 - core[0]), preferred_element_type=f32)


def combine_kernel(
    core, others, stats, labels, weight, received, target, n0, n1, n2, n3, gain,
    o0, o1, o2, o3, loss, marks, dlogit, held, inverse, factor
):
    sums = jnp.sum(stats[...], axis=0)
    total, picked = sums[0:4, :], sums[4:8, :]
    loss[...] = jnp.log(total) - picked
    slack = (jnp.exp(picked) / total - 1.0) * (1.0 - (picked / soft_cap) ** 2)
    scale = 1.0 / total
    marks[0:4, :] = scale
    marks[4:8, :] = slack
    for j in range(4):
        lines = slice(128 * j, 128 * (j + 1))
        inverse[lines, :] = turned_column(scale[j : j + 1, :])
        factor[lines, :] = turned_column(slack[j : j + 1, :])
        hit = hits_of(labels, j, (128, weight.shape[0]))
        rest = others[lines, :] * turned_column(scale[j : j + 1, :])
        dlogit[lines, :] = jnp.where(hit, turned_column(slack[j : j + 1, :]), rest).astype(bf16)
    for out in (o0, o1, o2, o3):
        out[:, half:] = jnp.zeros((block, 128), bf16)
    for j in range(tiles):
        lanes = slice(tile * j, tile * (j + 1))
        from_start = pl.ds(pl.multiple_of(core[0] * half + tile * j, tile), tile)
        held[j] = jnp.dot(dlogit[...], weight[:, from_start], preferred_element_type=f32)
        part = jnp.zeros((8, tile), f32)
        for d, (out, normed) in enumerate(((o0, n0), (o1, n1), (o2, n2), (o3, n3))):
            for k in range(4):
                at = pl.ds(pl.multiple_of(core[1 + 4 * d + k] * chunk, chunk), chunk)
                rows = slice(chunk * k, chunk * (k + 1))
                value = held[j, at, :] + received[at, lanes] * inverse[at, :]
                value += target[at, lanes].astype(f32) * factor[at, :]
                out[rows, lanes] = value.astype(bf16)
                value = value * normed[rows, lanes].astype(f32)
                part += jnp.sum(value.reshape(4, 8, tile), axis=0)
        sent = lane_rows(jnp.sum(part, axis=0, keepdims=True) / gain[:, from_start])
        high = sent.astype(bf16).astype(f32)
        sent = jnp.concatenate([high, sent - high], axis=0).astype(bf16)
        for out in (o0, o1, o2, o3):
            out[16 * j : 16 * (j + 1), half:] = sent


def head_kernel(core, others, marks, labels, n0, n1, n2, n3, m0, m1, m2, m3, out, turned, own, other):
    step = pl.program_id(0)

    @pl.when(step == 0)
    def _():
        for j in range(4):
            lines = slice(128 * j, 128 * (j + 1))
            rest = others[lines, :].T * marks[j : j + 1, :]
            hit = lax.broadcasted_iota(jnp.int32, rest.shape, 0) == labels[j : j + 1, :]
            turned[:, lines] = jnp.where(hit, marks[4 + j : 5 + j, :], rest).astype(bf16)
        for first, blocks, rows in ((1, (n0, n1, n2, n3), own), (1 + chunks, (m0, m1, m2, m3), other)):
            for d in range(4):
                for k in range(4):
                    row = pl.multiple_of(core[first + 4 * d + k] * chunk, chunk)
                    for j in range(tiles):
                        part = blocks[d][chunk * k : chunk * (k + 1), tile * j : tile * (j + 1)]
                        rows[j, pl.ds(row, chunk), :] = part

    near = step // tiles == core[0]

    @pl.when(near)
    def _():
        out[...] = jnp.dot(turned[...], own[step % tiles], preferred_element_type=f32).astype(bf16)

    @pl.when(jnp.logical_not(near))
    def _():
        out[...] = jnp.dot(turned[...], other[step % tiles], preferred_element_type=f32).astype(bf16)


def add_kernel(core, b0, b1, b2, b3, out):
    total = b0[...].astype(f32) + b1[...].astype(f32) + (b2[...].astype(f32) + b3[...].astype(f32))
    for j in range(tiles):
        out[:, wide * j : wide * j + tile] = total[:, tile * j : tile * (j + 1)].astype(bf16)
        rows = total[16 * j : 16 * j + 8, half:] + total[16 * j + 8 : 16 * j + 16, half:]
        rows = jnp.broadcast_to(rows[None], (plane, 8, 128)).reshape(block, 128)
        out[:, wide * j + tile : wide * (j + 1)] = rows.astype(bf16)


def sum_kernel(core, blocks, keep, send):
    total = jnp.sum(blocks[...].astype(f32), axis=0)
    first = core[0] == 0
    keep[...] = jnp.zeros_like(keep)
    send[...] = jnp.zeros_like(send)
    for j in range(tiles):
        lanes = slice(tile * j, tile * (j + 1))
        grad = total[:, wide * j : wide * j + tile]
        keep[0:4, lanes] = jnp.where(first, grad[:4], grad[4:])
        send[0:4, lanes] = jnp.where(first, grad[4:], grad[:4])
        for k in range(tile // 128):
            row = total[k : k + 1, wide * j + tile : wide * (j + 1)]
            lane = slice(tile * j + 128 * k, tile * j + 128 * (k + 1))
            keep[4:5, lane] = row
            send[4:5, lane] = row


def final_kernel(core, keep, received, unit, root, gain, loss, loss_out, grad_out, gain_out):
    line = loss[pl.ds(core[1 + 2 * chunks], 1), :]
    loss_out[...] = pltpu.roll(line, core[2 + 2 * chunks], 1)[0, :4]
    first = core[0] == 0
    near, far = keep[...], received[...]
    both = jnp.concatenate([jnp.where(first, near, far), jnp.where(first, far, near)], axis=1)
    gain_out[...] = both[4:5].reshape(width)
    grad_unit = both[0:4] * gain[...]
    rows = unit[...]
    inner = jnp.mean(grad_unit * rows, axis=1, keepdims=True)
    grad_out[...] = (grad_unit - rows * inner) / root[:, 0:1]


def call(kernel, core, args, out_shape, scratch=(), grid=(1,), out_specs=None, room=16):
    here = pl.BlockSpec(memory_space=pltpu.VMEM)
    return pl.pallas_call(
        kernel,
        grid_spec=pltpu.PrefetchScalarGridSpec(
            num_scalar_prefetch=1,
            grid=grid,
            in_specs=[here] * len(args),
            out_specs=out_specs or jax.tree.map(lambda _: here, out_shape),
            scratch_shapes=scratch,
        ),
        out_shape=out_shape,
        **params(room),
    )(core, *args)


def shape(dims, dtype):
    return jax.ShapeDtypeStruct(dims, dtype)


def body(hidden, norm_gain, weight, targets):
    vocab = weight.shape[0]
    place = [lax.axis_index(name) for name in every]
    device = ((place[0] * 2 + place[1]) * 4 + place[2]) * 4 + place[3]
    token = ((place[0] * 4 + place[2]) * 4 + place[3]) * 8 + place[1] * 4
    steps = jnp.arange(4, dtype=jnp.int32)
    by_x = ((place[0] + steps) % 4 * 4)[:, None] + steps[None, :]
    by_y = steps[None, :] * 4 + ((place[2] + steps) % 4)[:, None]
    first = place[1] == 0
    core = jnp.concatenate(
        [
            place[1][None],
            jnp.where(first, by_x, by_y).reshape(chunks),
            jnp.where(first, by_y, by_x).reshape(chunks),
            (token // 128)[None],
            ((128 - token % 128) % 128)[None],
            (device * vocab)[None],
        ]
    )
    gain = norm_gain

    spread, unit, root, gain = call(
        norm_kernel,
        core,
        (hidden, other_core(hidden), gain),
        [
            shape((plane, 8, half), bf16),
            shape((4, width), f32),
            shape((4, 128), f32),
            shape((1, width), f32),
        ],
    )
    near = over_plane(spread).reshape(block, half)
    sent = {d: along_line(near, -d) for d in (2, 1, 3)}
    near = [near, sent[1], sent[2], sent[3]]
    target, labels, part = call(
        first_logits_kernel,
        core,
        (weight, targets.reshape(4, 128), near[0]),
        [shape((tokens, half), bf16), shape((4, 128), jnp.int32), shape((block, vocab), f32)],
    )
    far = [other_core(near[0])]
    part, near[2], near[1], near[3] = lax.optimization_barrier((part, near[2], near[1], near[3]))
    target = other_core(target)
    sent = {d: other_core(near[d]) for d in (2, 1, 3)}
    far += [sent[1], sent[2], sent[3]]
    late_part = call(
        near_logits_kernel,
        core,
        (*near[1:], weight),
        shape((3 * block, vocab), f32),
        [pltpu.VMEM((3 * block, half), bf16)],
    )
    parts = [part, late_part]
    rest, stats, others = call(
        logits_kernel,
        core,
        (*far, weight, *parts, labels),
        [shape((tokens, vocab), f32), shape((8, 128), f32), shape((tokens, vocab), bf16)],
        [pltpu.VMEM((tokens, half), bf16)],
    )
    stats = stats + other_core(stats)
    far_grad = call(far_grad_kernel, core, (others, weight), shape((tokens, half), f32))
    stats, far_grad = lax.optimization_barrier((stats, far_grad))
    received = other_core(far_grad)
    stats = jnp.broadcast_to(stats[None], (n_chips, 8, 128))
    stats = lax.all_to_all(stats, chips, 0, 0, tiled=True)
    *sums, loss, marks = call(
        combine_kernel,
        core,
        (rest, stats, labels, weight, received, target, *near, gain),
        [shape((block, half + 128), bf16)] * 4 + [shape((4, 128), f32), shape((8, 128), f32)],
        [
            pltpu.VMEM((tokens, vocab), bf16),
            pltpu.VMEM((tiles, tokens, tile), f32),
            pltpu.VMEM((tokens, 1), f32),
            pltpu.VMEM((tokens, 1), f32),
        ],
    )
    arrived = [along_line(sums[d], d) for d in (1, 3, 2)]
    local = sums[0]
    grad_head = call(
        head_kernel,
        core,
        (rest, marks, labels, *near, *far),
        shape((vocab, width), bf16),
        [
            pltpu.VMEM((vocab, tokens), bf16),
            pltpu.VMEM((tiles, tokens, tile), bf16),
            pltpu.VMEM((tiles, tokens, tile), bf16),
        ],
        grid=(2 * tiles,),
        out_specs=pl.BlockSpec((vocab, tile), lambda j, c: (0, j)),
    )
    grad_head, local = lax.optimization_barrier((grad_head, local))
    packed = call(add_kernel, core, (local, *arrived), shape((block, tiles * wide), bf16))
    packed = over_plane(packed.reshape(plane, 8, tiles * wide))

    keep, send = call(sum_kernel, core, (packed,), [shape((8, half), f32)] * 2)
    token_loss, grad_hidden, grad_gain = call(
        final_kernel,
        core,
        (keep, other_core(send), unit, root, gain, loss),
        [shape((4,), f32), shape((4, width), f32), shape((width,), f32)],
    )
    return (token_loss, grad_gain, grad_hidden, grad_head)


def solution(mesh):
    fine = Mesh(mesh.devices.reshape(4, 2, 4, 4), every)
    rows = P(every, None)
    return jax.shard_map(
        body,
        mesh=fine,
        in_specs=(rows, P(), rows, P()),
        out_specs=(P(every), P(), rows, rows),
        check_vma=False,
    )
```

```python
import jax
import jax.numpy as jnp
from jax import lax
from jax.experimental import pallas as pl
from jax.experimental.pallas import tpu as pltpu
from jax.sharding import Mesh
from jax.sharding import PartitionSpec as P

soft_cap = 30.0
norm_eps = 1e-06
f32 = jnp.float32
bf16 = jnp.bfloat16
every = ("x", "c", "y", "z")
chips = ("x", "y", "z")
n_chips = 64
tokens = 512
width = 4608
half = width // 2
tile = 768
tiles = half // tile
wide = tile + 128

plane = 16
vocab_tile = 256
block = tokens // 4
chunk = 32
chunks = tokens // chunk


def index(x, c, y, z):
    return ((x % 4 * 2 + c % 2) * 4 + y % 4) * 4 + z % 4


places = [(x, c, y, z) for x in range(4) for c in range(2) for y in range(4) for z in range(4)]
swap_cores = [(index(x, c, y, z), index(x, c + 1, y, z)) for x, c, y, z in places]
planes = [[index(x, 0, y, z) for y in range(4) for z in range(4)] for x in range(4)]
planes += [[index(x, 1, y, z) for x in range(4) for z in range(4)] for y in range(4)]


def other_core(array):
    return lax.ppermute(array, every, swap_cores)


def along_line(array, step):
    pairs = [
        (index(x, c, y, z), index(x + step * (1 - c), c, y + step * c, z)) for x, c, y, z in places
    ]
    return lax.ppermute(array, every, pairs)


def over_plane(array):
    return lax.all_to_all(array, every, 0, 0, axis_index_groups=planes, tiled=True)


def lane_rows(part):
    rows = [part[:, 128 * j : 128 * (j + 1)] for j in range(tile // 128)]
    return jnp.concatenate(rows + [jnp.zeros((8 - len(rows), 128), f32)], axis=0)


def assemble(table, blocks, out):
    for d in range(4):
        for k in range(4):
            row = pl.multiple_of(table(4 * d + k) * chunk, chunk)
            out[pl.ds(row, chunk), :] = blocks[d][chunk * k : chunk * (k + 1), :]


def params(room):
    return dict(
        compiler_params=pltpu.CompilerParams(vmem_limit_bytes=room << 20),
        cost_estimate=pl.CostEstimate(flops=1000, bytes_accessed=1000, transcendentals=0),
    )


def norm_kernel(core, mine, theirs, gain, spread, unit_out, root_out, row):
    first = core[0] == 0
    own = mine[...].astype(f32)
    far = theirs[...].astype(f32)
    rows = jnp.concatenate([jnp.where(first, own, far), jnp.where(first, far, own)], axis=0)
    root = jnp.sqrt(jnp.mean(rows * rows, axis=1, keepdims=True) + norm_eps)
    unit = rows / root
    normed = unit * gain[...].reshape(1, width)
    part = jnp.where(first, normed[:, :half], normed[:, half:]).astype(bf16)
    row[...] = gain[...].reshape(1, width)
    spread[...] = jnp.broadcast_to(part[None], spread.shape)
    unit_out[...] = jnp.where(first, unit[:4], unit[4:])
    root_out[...] = jnp.broadcast_to(jnp.where(first, root[:4], root[4:]), root_out.shape)


def half_of(weight, which):
    return weight[:, pl.ds(pl.multiple_of(which * half, half), half)]


def turned_column(row):
    return jnp.broadcast_to(row, (128, 128)).T[:, 0:1]


def hits_of(labels, j, dims):
    label = turned_column(labels[j : j + 1, :].astype(f32)).astype(jnp.int32)
    return lax.broadcasted_iota(jnp.int32, dims, 1) == label


def onehot_rows(labels, vocab):
    rows = [hits_of(labels, j, (128, vocab)).astype(f32).astype(bf16) for j in range(4)]
    return jnp.concatenate(rows, axis=0)


def first_logits_kernel(core, weight, targets, b0, out, labels, part):
    to = lax.broadcasted_iota(jnp.int32, (128, 128), 1)
    source = ((to >> 2) & 1) * 64 + (to >> 3) * 4 + (to & 3)
    order = (lax.broadcasted_iota(jnp.int32, (128, 128), 0) == source).astype(f32)
    ids = jnp.concatenate([targets[...].astype(f32), jnp.zeros((4, 128), f32)], axis=0)
    ids = jnp.dot(ids, order, precision=lax.Precision.HIGHEST, preferred_element_type=f32)
    labels[...] = ids[:4].astype(jnp.int32) - core[3 + 2 * chunks]
    onehot = onehot_rows(labels, weight.shape[0])
    out[...] = jnp.dot(
        onehot, half_of(weight, 1 - core[0]), preferred_element_type=f32
    ).astype(bf16)
    part[...] = lax.dot_general(
        b0[...], half_of(weight, core[0]), (((1,), (1,)), ((), ())), preferred_element_type=f32
    )


def near_logits_kernel(core, *refs):
    *blocks, weight, out, rows = refs
    for d, ref in enumerate(blocks):
        rows[block * d : block * (d + 1), :] = ref[...]
    out[...] = lax.dot_general(
        rows[...], half_of(weight, core[0]), (((1,), (1,)), ((), ())), preferred_element_type=f32
    )


def logits_kernel(
    core, b0, b1, b2, b3, weight, part0, part1, labels, out, stats, others, rows
):
    assemble(lambda i: core[1 + chunks + i], (b0, b1, b2, b3), rows)
    vocab = weight.shape[0]
    from_start = pl.ds(pl.multiple_of((1 - core[0]) * half, half), half)
    marks = [turned_column(labels[j : j + 1, :].astype(f32)).astype(jnp.int32) for j in range(4)]
    totals = [jnp.zeros((128, 1), f32)] * 4
    picks = [jnp.zeros((128, 1), f32)] * 4
    for start in range(0, vocab, vocab_tile):
        some = slice(start, min(start + vocab_tile, vocab))
        out[:, some] = lax.dot_general(
            rows[...], weight[some, from_start], (((1,), (1,)), ((), ())), preferred_element_type=f32
        )
        for i in range(chunks):
            row = pl.multiple_of(core[1 + i] * chunk, chunk)
            part, at = (part0, i) if i < 4 else (part1, i - 4)
            out[pl.ds(row, chunk), some] += part[chunk * at : chunk * (at + 1), some]
        for j in range(4):
            lines = slice(128 * j, 128 * (j + 1))
            capped = soft_cap * jnp.tanh(out[lines, some] / soft_cap)
            hit = lax.broadcasted_iota(jnp.int32, capped.shape, 1) + start == marks[j]
            exps = jnp.exp(capped)
            slope = 1.0 - (capped / soft_cap) ** 2
            rest = jnp.where(hit, 0.0, exps * slope)
            out[lines, some] = rest
            others[lines, some] = rest.astype(bf16)
            totals[j] = totals[j] + jnp.sum(exps, axis=1, keepdims=True)
            picked = jnp.where(hit, capped, 0.0)
            picks[j] = picks[j] + jnp.sum(picked, axis=1, keepdims=True)
    for j in range(4):
        stats[j : j + 1, :] = jnp.broadcast_to(totals[j], (128, 128)).T[0:1, :]
        stats[4 + j : 5 + j, :] = jnp.broadcast_to(picks[j], (128, 128)).T[0:1, :]


def far_grad_kernel(core, others, weight, out):
    out[...] = jnp.dot(others[...], half_of(weight, 1 - core[0]), preferred_element_type=f32)


def combine_kernel(
    core, others, stats, labels, weight, received, target, n0, n1, n2, n3, gain,
    o0, o1, o2, o3, loss, marks, dlogit, held, inverse, factor
):
    sums = jnp.sum(stats[...], axis=0)
    total, picked = sums[0:4, :], sums[4:8, :]
    loss[...] = jnp.log(total) - picked
    slack = (jnp.exp(picked) / total - 1.0) * (1.0 - (picked / soft_cap) ** 2)
    scale = 1.0 / total
    marks[0:4, :] = scale
    marks[4:8, :] = slack
    for j in range(4):
        lines = slice(128 * j, 128 * (j + 1))
        inverse[lines, :] = turned_column(scale[j : j + 1, :])
        factor[lines, :] = turned_column(slack[j : j + 1, :])
        hit = hits_of(labels, j, (128, weight.shape[0]))
        rest = others[lines, :] * turned_column(scale[j : j + 1, :])
        dlogit[lines, :] = jnp.where(hit, turned_column(slack[j : j + 1, :]), rest).astype(bf16)
    for out in (o0, o1, o2, o3):
        out[:, half:] = jnp.zeros((block, 128), bf16)
    for j in range(tiles):
        lanes = slice(tile * j, tile * (j + 1))
        from_start = pl.ds(pl.multiple_of(core[0] * half + tile * j, tile), tile)
        held[j] = jnp.dot(dlogit[...], weight[:, from_start], preferred_element_type=f32)
        part = jnp.zeros((8, tile), f32)
        for d, (out, normed) in enumerate(((o0, n0), (o1, n1), (o2, n2), (o3, n3))):
            for k in range(4):
                at = pl.ds(pl.multiple_of(core[1 + 4 * d + k] * chunk, chunk), chunk)
                rows = slice(chunk * k, chunk * (k + 1))
                value = held[j, at, :] + received[at, lanes] * inverse[at, :]
                value += target[at, lanes].astype(f32) * factor[at, :]
                out[rows, lanes] = value.astype(bf16)
                value = value * normed[rows, lanes].astype(f32)
                part += jnp.sum(value.reshape(4, 8, tile), axis=0)
        sent = lane_rows(jnp.sum(part, axis=0, keepdims=True) / gain[:, from_start])
        high = sent.astype(bf16).astype(f32)
        sent = jnp.concatenate([high, sent - high], axis=0).astype(bf16)
        for out in (o0, o1, o2, o3):
            out[16 * j : 16 * (j + 1), half:] = sent


def head_kernel(core, others, marks, labels, n0, n1, n2, n3, m0, m1, m2, m3, out, turned, own, other):
    step = pl.program_id(0)

    @pl.when(step == 0)
    def _():
        for j in range(4):
            lines = slice(128 * j, 128 * (j + 1))
            rest = others[lines, :].T * marks[j : j + 1, :]
            hit = lax.broadcasted_iota(jnp.int32, rest.shape, 0) == labels[j : j + 1, :]
            turned[:, lines] = jnp.where(hit, marks[4 + j : 5 + j, :], rest).astype(bf16)
        for first, blocks, rows in ((1, (n0, n1, n2, n3), own), (1 + chunks, (m0, m1, m2, m3), other)):
            for d in range(4):
                for k in range(4):
                    row = pl.multiple_of(core[first + 4 * d + k] * chunk, chunk)
                    for j in range(tiles):
                        part = blocks[d][chunk * k : chunk * (k + 1), tile * j : tile * (j + 1)]
                        rows[j, pl.ds(row, chunk), :] = part

    near = step // tiles == core[0]

    @pl.when(near)
    def _():
        out[...] = jnp.dot(turned[...], own[step % tiles], preferred_element_type=f32).astype(bf16)

    @pl.when(jnp.logical_not(near))
    def _():
        out[...] = jnp.dot(turned[...], other[step % tiles], preferred_element_type=f32).astype(bf16)


def add_kernel(core, b0, b1, b2, b3, out):
    total = b0[...].astype(f32) + b1[...].astype(f32) + (b2[...].astype(f32) + b3[...].astype(f32))
    for j in range(tiles):
        out[:, wide * j : wide * j + tile] = total[:, tile * j : tile * (j + 1)].astype(bf16)
        rows = total[16 * j : 16 * j + 8, half:] + total[16 * j + 8 : 16 * j + 16, half:]
        rows = jnp.broadcast_to(rows[None], (plane, 8, 128)).reshape(block, 128)
        out[:, wide * j + tile : wide * (j + 1)] = rows.astype(bf16)


def sum_kernel(core, blocks, keep, send):
    total = jnp.sum(blocks[...].astype(f32), axis=0)
    first = core[0] == 0
    keep[...] = jnp.zeros_like(keep)
    send[...] = jnp.zeros_like(send)
    for j in range(tiles):
        lanes = slice(tile * j, tile * (j + 1))
        grad = total[:, wide * j : wide * j + tile]
        keep[0:4, lanes] = jnp.where(first, grad[:4], grad[4:])
        send[0:4, lanes] = jnp.where(first, grad[4:], grad[:4])
        for k in range(tile // 128):
            row = total[k : k + 1, wide * j + tile : wide * (j + 1)]
            lane = slice(tile * j + 128 * k, tile * j + 128 * (k + 1))
            keep[4:5, lane] = row
            send[4:5, lane] = row


def final_kernel(core, keep, received, unit, root, gain, loss, loss_out, grad_out, gain_out):
    line = loss[pl.ds(core[1 + 2 * chunks], 1), :]
    loss_out[...] = pltpu.roll(line, core[2 + 2 * chunks], 1)[0, :4]
    first = core[0] == 0
    near, far = keep[...], received[...]
    both = jnp.concatenate([jnp.where(first, near, far), jnp.where(first, far, near)], axis=1)
    gain_out[...] = both[4:5].reshape(width)
    grad_unit = both[0:4] * gain[...]
    rows = unit[...]
    inner = jnp.mean(grad_unit * rows, axis=1, keepdims=True)
    grad_out[...] = (grad_unit - rows * inner) / root[:, 0:1]


def call(kernel, core, args, out_shape, scratch=(), grid=(1,), out_specs=None, room=16):
    here = pl.BlockSpec(memory_space=pltpu.VMEM)
    return pl.pallas_call(
        kernel,
        grid_spec=pltpu.PrefetchScalarGridSpec(
            num_scalar_prefetch=1,
            grid=grid,
            in_specs=[here] * len(args),
            out_specs=out_specs or jax.tree.map(lambda _: here, out_shape),
            scratch_shapes=scratch,
        ),
        out_shape=out_shape,
        **params(room),
    )(core, *args)


def shape(dims, dtype):
    return jax.ShapeDtypeStruct(dims, dtype)


def body(hidden, norm_gain, weight, targets):
    vocab = weight.shape[0]
    place = [lax.axis_index(name) for name in every]
    device = ((place[0] * 2 + place[1]) * 4 + place[2]) * 4 + place[3]
    token = ((place[0] * 4 + place[2]) * 4 + place[3]) * 8 + place[1] * 4
    steps = jnp.arange(4, dtype=jnp.int32)
    by_x = ((place[0] + steps) % 4 * 4)[:, None] + steps[None, :]
    by_y = steps[None, :] * 4 + ((place[2] + steps) % 4)[:, None]
    first = place[1] == 0
    core = jnp.concatenate(
        [
            place[1][None],
            jnp.where(first, by_x, by_y).reshape(chunks),
            jnp.where(first, by_y, by_x).reshape(chunks),
            (token // 128)[None],
            ((128 - token % 128) % 128)[None],
            (device * vocab)[None],
        ]
    )
    gain = norm_gain

    spread, unit, root, gain = call(
        norm_kernel,
        core,
        (hidden, other_core(hidden), gain),
        [
            shape((plane, 8, half), bf16),
            shape((4, width), f32),
            shape((4, 128), f32),
            shape((1, width), f32),
        ],
    )
    near = over_plane(spread).reshape(block, half)
    sent = {d: along_line(near, -d) for d in (3, 1, 2)}
    near = [near, sent[1], sent[2], sent[3]]
    target, labels, part = call(
        first_logits_kernel,
        core,
        (weight, targets.reshape(4, 128), near[0]),
        [shape((tokens, half), bf16), shape((4, 128), jnp.int32), shape((block, vocab), f32)],
    )
    far = [other_core(near[0])]
    part, near[2], near[1], near[3] = lax.optimization_barrier((part, near[2], near[1], near[3]))
    target = other_core(target)
    sent = {d: other_core(near[d]) for d in (2, 1, 3)}
    far += [sent[1], sent[2], sent[3]]
    late_part = call(
        near_logits_kernel,
        core,
        (*near[1:], weight),
        shape((3 * block, vocab), f32),
        [pltpu.VMEM((3 * block, half), bf16)],
    )
    parts = [part, late_part]
    rest, stats, others = call(
        logits_kernel,
        core,
        (*far, weight, *parts, labels),
        [shape((tokens, vocab), f32), shape((8, 128), f32), shape((tokens, vocab), bf16)],
        [pltpu.VMEM((tokens, half), bf16)],
    )
    stats = stats + other_core(stats)
    far_grad = call(far_grad_kernel, core, (others, weight), shape((tokens, half), f32))
    stats, far_grad = lax.optimization_barrier((stats, far_grad))
    received = other_core(far_grad)
    stats = jnp.broadcast_to(stats[None], (n_chips, 8, 128))
    stats = lax.all_to_all(stats, chips, 0, 0, tiled=True)
    *sums, loss, marks = call(
        combine_kernel,
        core,
        (rest, stats, labels, weight, received, target, *near, gain),
        [shape((block, half + 128), bf16)] * 4 + [shape((4, 128), f32), shape((8, 128), f32)],
        [
            pltpu.VMEM((tokens, vocab), bf16),
            pltpu.VMEM((tiles, tokens, tile), f32),
            pltpu.VMEM((tokens, 1), f32),
            pltpu.VMEM((tokens, 1), f32),
        ],
    )
    arrived = [along_line(sums[d], d) for d in (1, 3, 2)]
    local = sums[0]
    grad_head = call(
        head_kernel,
        core,
        (rest, marks, labels, *near, *far),
        shape((vocab, width), bf16),
        [
            pltpu.VMEM((vocab, tokens), bf16),
            pltpu.VMEM((tiles, tokens, tile), bf16),
            pltpu.VMEM((tiles, tokens, tile), bf16),
        ],
        grid=(2 * tiles,),
        out_specs=pl.BlockSpec((vocab, tile), lambda j, c: (0, j)),
    )
    grad_head, local = lax.optimization_barrier((grad_head, local))
    packed = call(add_kernel, core, (local, *arrived), shape((block, tiles * wide), bf16))
    packed = over_plane(packed.reshape(plane, 8, tiles * wide))

    keep, send = call(sum_kernel, core, (packed,), [shape((8, half), f32)] * 2)
    token_loss, grad_hidden, grad_gain = call(
        final_kernel,
        core,
        (keep, other_core(send), unit, root, gain, loss),
        [shape((4,), f32), shape((4, width), f32), shape((width,), f32)],
    )
    return (token_loss, grad_gain, grad_hidden, grad_head)


def solution(mesh):
    fine = Mesh(mesh.devices.reshape(4, 2, 4, 4), every)
    rows = P(every, None)
    return jax.shard_map(
        body,
        mesh=fine,
        in_specs=(rows, P(), rows, P()),
        out_specs=(P(every), P(), rows, rows),
        check_vma=False,
    )
```

```python
import jax
import jax.numpy as jnp
from jax import lax
from jax.experimental import pallas as pl
from jax.experimental.pallas import tpu as pltpu
from jax.sharding import Mesh
from jax.sharding import PartitionSpec as P

soft_cap = 30.0
norm_eps = 1e-06
f32 = jnp.float32
bf16 = jnp.bfloat16
every = ("x", "c", "y", "z")
chips = ("x", "y", "z")
n_chips = 64
tokens = 512
width = 4608
half = width // 2
tile = 768
tiles = half // tile
wide = tile + 128

plane = 16
vocab_tile = 256
block = tokens // 4
chunk = 32
chunks = tokens // chunk


def index(x, c, y, z):
    return ((x % 4 * 2 + c % 2) * 4 + y % 4) * 4 + z % 4


places = [(x, c, y, z) for x in range(4) for c in range(2) for y in range(4) for z in range(4)]
swap_cores = [(index(x, c, y, z), index(x, c + 1, y, z)) for x, c, y, z in places]
planes = [[index(x, 0, y, z) for y in range(4) for z in range(4)] for x in range(4)]
planes += [[index(x, 1, y, z) for x in range(4) for z in range(4)] for y in range(4)]


def other_core(array):
    return lax.ppermute(array, every, swap_cores)


def along_line(array, step):
    pairs = [
        (index(x, c, y, z), index(x + step * (1 - c), c, y + step * c, z)) for x, c, y, z in places
    ]
    return lax.ppermute(array, every, pairs)


def over_plane(array):
    return lax.all_to_all(array, every, 0, 0, axis_index_groups=planes, tiled=True)


def lane_rows(part):
    rows = [part[:, 128 * j : 128 * (j + 1)] for j in range(tile // 128)]
    return jnp.concatenate(rows + [jnp.zeros((8 - len(rows), 128), f32)], axis=0)


def assemble(table, blocks, out):
    for d in range(4):
        for k in range(4):
            row = pl.multiple_of(table(4 * d + k) * chunk, chunk)
            out[pl.ds(row, chunk), :] = blocks[d][chunk * k : chunk * (k + 1), :]


def params(room):
    return dict(
        compiler_params=pltpu.CompilerParams(vmem_limit_bytes=room << 20),
        cost_estimate=pl.CostEstimate(flops=1000, bytes_accessed=1000, transcendentals=0),
    )


def norm_kernel(core, mine, theirs, gain, spread, unit_out, root_out, row):
    first = core[0] == 0
    own = mine[...].astype(f32)
    far = theirs[...].astype(f32)
    rows = jnp.concatenate([jnp.where(first, own, far), jnp.where(first, far, own)], axis=0)
    root = jnp.sqrt(jnp.mean(rows * rows, axis=1, keepdims=True) + norm_eps)
    unit = rows / root
    normed = unit * gain[...].reshape(1, width)
    part = jnp.where(first, normed[:, :half], normed[:, half:]).astype(bf16)
    row[...] = gain[...].reshape(1, width)
    spread[...] = jnp.broadcast_to(part[None], spread.shape)
    unit_out[...] = jnp.where(first, unit[:4], unit[4:])
    root_out[...] = jnp.broadcast_to(jnp.where(first, root[:4], root[4:]), root_out.shape)


def half_of(weight, which):
    return weight[:, pl.ds(pl.multiple_of(which * half, half), half)]


def turned_column(row):
    return jnp.broadcast_to(row, (128, 128)).T[:, 0:1]


def hits_of(labels, j, dims):
    label = turned_column(labels[j : j + 1, :].astype(f32)).astype(jnp.int32)
    return lax.broadcasted_iota(jnp.int32, dims, 1) == label


def onehot_rows(labels, vocab):
    rows = [hits_of(labels, j, (128, vocab)).astype(f32).astype(bf16) for j in range(4)]
    return jnp.concatenate(rows, axis=0)


def far_target_kernel(core, weight, labels, out):
    onehot = onehot_rows(labels, weight.shape[0])
    out[...] = jnp.dot(
        onehot, half_of(weight, 1 - core[0]), preferred_element_type=f32
    ).astype(bf16)


def near_logits_kernel(core, *refs):
    *blocks, weight, out, rows = refs
    for d, ref in enumerate(blocks):
        rows[block * d : block * (d + 1), :] = ref[...]
    out[...] = lax.dot_general(
        rows[...], half_of(weight, core[0]), (((1,), (1,)), ((), ())), preferred_element_type=f32
    )


def logits_kernel(
    core, b0, b1, b2, b3, weight, part0, part1, labels, out, stats, others, rows
):
    assemble(lambda i: core[1 + chunks + i], (b0, b1, b2, b3), rows)
    vocab = weight.shape[0]
    from_start = pl.ds(pl.multiple_of((1 - core[0]) * half, half), half)
    marks = [turned_column(labels[j : j + 1, :].astype(f32)).astype(jnp.int32) for j in range(4)]
    totals = [jnp.zeros((128, 1), f32)] * 4
    picks = [jnp.zeros((128, 1), f32)] * 4
    for start in range(0, vocab, vocab_tile):
        some = slice(start, min(start + vocab_tile, vocab))
        out[:, some] = lax.dot_general(
            rows[...], weight[some, from_start], (((1,), (1,)), ((), ())), preferred_element_type=f32
        )
        for i in range(chunks):
            row = pl.multiple_of(core[1 + i] * chunk, chunk)
            part, at = (part0, i) if i < 4 else (part1, i - 4)
            out[pl.ds(row, chunk), some] += part[chunk * at : chunk * (at + 1), some]
        for j in range(4):
            lines = slice(128 * j, 128 * (j + 1))
            level = jnp.tanh(out[lines, some] * (1.0 / soft_cap))
            capped = soft_cap * level
            hit = lax.broadcasted_iota(jnp.int32, capped.shape, 1) + start == marks[j]
            exps = jnp.exp(capped)
            slope = 1.0 - level * level
            rest = jnp.where(hit, 0.0, exps * slope)
            out[lines, some] = rest
            others[lines, some] = rest.astype(bf16)
            totals[j] = totals[j] + jnp.sum(exps, axis=1, keepdims=True)
            picked = jnp.where(hit, capped, 0.0)
            picks[j] = picks[j] + jnp.sum(picked, axis=1, keepdims=True)
    for j in range(4):
        stats[j : j + 1, :] = jnp.broadcast_to(totals[j], (128, 128)).T[0:1, :]
        stats[4 + j : 5 + j, :] = jnp.broadcast_to(picks[j], (128, 128)).T[0:1, :]


def far_grad_kernel(core, others, weight, out):
    grad = jnp.dot(others[...], half_of(weight, 1 - core[0]), preferred_element_type=f32)
    out[...] = grad.astype(bf16)


def combine_kernel(
    core, others, stats, labels, weight, received, target, n0, n1, n2, n3, gain,
    o0, o1, o2, o3, loss, marks, dlogit, held, inverse, factor
):
    sums = jnp.sum(stats[...], axis=0)
    total, picked = sums[0:4, :], sums[4:8, :]
    loss[...] = jnp.log(total) - picked
    slack = (jnp.exp(picked) / total - 1.0) * (1.0 - (picked / soft_cap) ** 2)
    scale = 1.0 / total
    marks[0:4, :] = scale
    marks[4:8, :] = slack
    for j in range(4):
        lines = slice(128 * j, 128 * (j + 1))
        inverse[lines, :] = turned_column(scale[j : j + 1, :])
        factor[lines, :] = turned_column(slack[j : j + 1, :])
        hit = hits_of(labels, j, (128, weight.shape[0]))
        rest = others[lines, :] * turned_column(scale[j : j + 1, :])
        dlogit[lines, :] = jnp.where(hit, turned_column(slack[j : j + 1, :]), rest).astype(bf16)
    for out in (o0, o1, o2, o3):
        out[:, half:] = jnp.zeros((block, 128), bf16)
    for j in range(tiles):
        lanes = slice(tile * j, tile * (j + 1))
        from_start = pl.ds(pl.multiple_of(core[0] * half + tile * j, tile), tile)
        held[j] = jnp.dot(dlogit[...], weight[:, from_start], preferred_element_type=f32)
        part = jnp.zeros((8, tile), f32)
        for d, (out, normed) in enumerate(((o0, n0), (o1, n1), (o2, n2), (o3, n3))):
            for k in range(4):
                at = pl.ds(pl.multiple_of(core[1 + 4 * d + k] * chunk, chunk), chunk)
                rows = slice(chunk * k, chunk * (k + 1))
                value = held[j, at, :] + received[at, lanes].astype(f32) * inverse[at, :]
                value += target[at, lanes].astype(f32) * factor[at, :]
                out[rows, lanes] = value.astype(bf16)
                value = value * normed[rows, lanes].astype(f32)
                part += jnp.sum(value.reshape(4, 8, tile), axis=0)
        sent = lane_rows(jnp.sum(part, axis=0, keepdims=True) / gain[:, from_start])
        high = sent.astype(bf16).astype(f32)
        sent = jnp.concatenate([high, sent - high], axis=0).astype(bf16)
        for out in (o0, o1, o2, o3):
            out[16 * j : 16 * (j + 1), half:] = sent


def head_kernel(core, others, marks, labels, n0, n1, n2, n3, m0, m1, m2, m3, out, turned, own, other):
    step = pl.program_id(0)

    @pl.when(step == 0)
    def _():
        for j in range(4):
            lines = slice(128 * j, 128 * (j + 1))
            rest = others[lines, :].T * marks[j : j + 1, :]
            hit = lax.broadcasted_iota(jnp.int32, rest.shape, 0) == labels[j : j + 1, :]
            turned[:, lines] = jnp.where(hit, marks[4 + j : 5 + j, :], rest).astype(bf16)
        for first, blocks, rows in ((1, (n0, n1, n2, n3), own), (1 + chunks, (m0, m1, m2, m3), other)):
            for d in range(4):
                for k in range(4):
                    row = pl.multiple_of(core[first + 4 * d + k] * chunk, chunk)
                    for j in range(tiles):
                        part = blocks[d][chunk * k : chunk * (k + 1), tile * j : tile * (j + 1)]
                        rows[j, pl.ds(row, chunk), :] = part

    near = step // tiles == core[0]

    @pl.when(near)
    def _():
        out[...] = jnp.dot(turned[...], own[step % tiles], preferred_element_type=f32).astype(bf16)

    @pl.when(jnp.logical_not(near))
    def _():
        out[...] = jnp.dot(turned[...], other[step % tiles], preferred_element_type=f32).astype(bf16)


def add_kernel(core, b0, b1, b2, b3, out):
    total = b0[...].astype(f32) + b1[...].astype(f32) + (b2[...].astype(f32) + b3[...].astype(f32))
    for j in range(tiles):
        out[:, wide * j : wide * j + tile] = total[:, tile * j : tile * (j + 1)].astype(bf16)
        rows = total[16 * j : 16 * j + 8, half:] + total[16 * j + 8 : 16 * j + 16, half:]
        rows = jnp.broadcast_to(rows[None], (plane, 8, 128)).reshape(block, 128)
        out[:, wide * j + tile : wide * (j + 1)] = rows.astype(bf16)


def sum_kernel(core, blocks, keep, send):
    total = jnp.sum(blocks[...].astype(f32), axis=0)
    first = core[0] == 0
    keep[...] = jnp.zeros_like(keep)
    send[...] = jnp.zeros_like(send)
    for j in range(tiles):
        lanes = slice(tile * j, tile * (j + 1))
        grad = total[:, wide * j : wide * j + tile]
        keep[0:4, lanes] = jnp.where(first, grad[:4], grad[4:])
        send[0:4, lanes] = jnp.where(first, grad[4:], grad[:4])
        for k in range(tile // 128):
            row = total[k : k + 1, wide * j + tile : wide * (j + 1)]
            lane = slice(tile * j + 128 * k, tile * j + 128 * (k + 1))
            keep[4:5, lane] = row
            send[4:5, lane] = row


def final_kernel(core, keep, received, unit, root, gain, loss, loss_out, grad_out, gain_out):
    line = loss[pl.ds(core[1 + 2 * chunks], 1), :]
    loss_out[...] = pltpu.roll(line, core[2 + 2 * chunks], 1)[0, :4]
    first = core[0] == 0
    near, far = keep[...], received[...]
    both = jnp.concatenate([jnp.where(first, near, far), jnp.where(first, far, near)], axis=1)
    gain_out[...] = both[4:5].reshape(width)
    grad_unit = both[0:4] * gain[...]
    rows = unit[...]
    inner = jnp.mean(grad_unit * rows, axis=1, keepdims=True)
    grad_out[...] = (grad_unit - rows * inner) / root[:, 0:1]


def call(kernel, core, args, out_shape, scratch=(), grid=(1,), out_specs=None, room=16):
    here = pl.BlockSpec(memory_space=pltpu.VMEM)
    return pl.pallas_call(
        kernel,
        grid_spec=pltpu.PrefetchScalarGridSpec(
            num_scalar_prefetch=1,
            grid=grid,
            in_specs=[here] * len(args),
            out_specs=out_specs or jax.tree.map(lambda _: here, out_shape),
            scratch_shapes=scratch,
        ),
        out_shape=out_shape,
        **params(room),
    )(core, *args)


def shape(dims, dtype):
    return jax.ShapeDtypeStruct(dims, dtype)


def body(hidden, norm_gain, weight, targets):
    vocab = weight.shape[0]
    place = [lax.axis_index(name) for name in every]
    device = ((place[0] * 2 + place[1]) * 4 + place[2]) * 4 + place[3]
    token = ((place[0] * 4 + place[2]) * 4 + place[3]) * 8 + place[1] * 4
    steps = jnp.arange(4, dtype=jnp.int32)
    by_x = ((place[0] + steps) % 4 * 4)[:, None] + steps[None, :]
    by_y = steps[None, :] * 4 + ((place[2] + steps) % 4)[:, None]
    first = place[1] == 0
    core = jnp.concatenate(
        [
            place[1][None],
            jnp.where(first, by_x, by_y).reshape(chunks),
            jnp.where(first, by_y, by_x).reshape(chunks),
            (token // 128)[None],
            ((128 - token % 128) % 128)[None],
        ]
    )
    gain = norm_gain

    labels = targets.reshape(4, 2, 16, 4).transpose(0, 2, 1, 3).reshape(4, 128) - device * vocab
    spread, unit, root, gain = call(
        norm_kernel,
        core,
        (hidden, other_core(hidden), gain),
        [
            shape((plane, 8, half), bf16),
            shape((4, width), f32),
            shape((4, 128), f32),
            shape((1, width), f32),
        ],
    )
    spread, labels = lax.optimization_barrier((spread, labels))
    near = over_plane(spread).reshape(block, half)
    sent = {d: along_line(near, -d) for d in (2, 1, 3)}
    near = [near, sent[1], sent[2], sent[3]]
    local, late = lax.optimization_barrier((near[0], labels))
    target = call(far_target_kernel, core, (weight, late), shape((tokens, half), bf16))
    local, target = lax.optimization_barrier((local, target))
    target = other_core(target)
    parts = []
    far = [None] * 4
    for group in ((0,), (1, 2, 3)):
        for d in (0,) if group == (0,) else (2, 1, 3):
            far[d] = other_core(near[d])
        part = call(
            near_logits_kernel,
            core,
            (*(near[d] if d else local for d in group), weight),
            shape((len(group) * block, vocab), f32),
            [pltpu.VMEM((len(group) * block, half), bf16)],
        )
        if group[0] == 0:
            part, near[2], near[1], near[3] = lax.optimization_barrier(
                (part, near[2], near[1], near[3])
            )
        parts.append(part)
    rest, stats, others = call(
        logits_kernel,
        core,
        (*far, weight, *parts, labels),
        [shape((tokens, vocab), f32), shape((8, 128), f32), shape((tokens, vocab), bf16)],
        [pltpu.VMEM((tokens, half), bf16)],
    )
    stats = stats + other_core(stats)
    far_grad = call(far_grad_kernel, core, (others, weight), shape((tokens, half), bf16))
    stats, far_grad = lax.optimization_barrier((stats, far_grad))
    received = other_core(far_grad)
    stats = jnp.broadcast_to(stats[None], (n_chips, 8, 128))
    stats = lax.all_to_all(stats, chips, 0, 0, tiled=True)
    *sums, loss, marks = call(
        combine_kernel,
        core,
        (rest, stats, labels, weight, received, target, *near, gain),
        [shape((block, half + 128), bf16)] * 4 + [shape((4, 128), f32), shape((8, 128), f32)],
        [
            pltpu.VMEM((tokens, vocab), bf16),
            pltpu.VMEM((tiles, tokens, tile), f32),
            pltpu.VMEM((tokens, 1), f32),
            pltpu.VMEM((tokens, 1), f32),
        ],
    )
    arrived = [along_line(sums[d], d) for d in (1, 3, 2)]
    local = sums[0]
    grad_head = call(
        head_kernel,
        core,
        (rest, marks, labels, *near, *far),
        shape((vocab, width), bf16),
        [
            pltpu.VMEM((vocab, tokens), bf16),
            pltpu.VMEM((tiles, tokens, tile), bf16),
            pltpu.VMEM((tiles, tokens, tile), bf16),
        ],
        grid=(2 * tiles,),
        out_specs=pl.BlockSpec((vocab, tile), lambda j, c: (0, j)),
    )
    grad_head, local = lax.optimization_barrier((grad_head, local))
    packed = call(add_kernel, core, (local, *arrived), shape((block, tiles * wide), bf16))
    packed = over_plane(packed.reshape(plane, 8, tiles * wide))

    keep, send = call(sum_kernel, core, (packed,), [shape((8, half), f32)] * 2)
    token_loss, grad_hidden, grad_gain = call(
        final_kernel,
        core,
        (keep, other_core(send), unit, root, gain, loss),
        [shape((4,), f32), shape((4, width), f32), shape((width,), f32)],
    )
    return (token_loss, grad_gain, grad_hidden, grad_head)


def solution(mesh):
    fine = Mesh(mesh.devices.reshape(4, 2, 4, 4), every)
    rows = P(every, None)
    return jax.shard_map(
        body,
        mesh=fine,
        in_specs=(rows, P(), rows, P()),
        out_specs=(P(every), P(), rows, rows),
        check_vma=False,
    )
```
